128 devices in a mesh: row: 16 (over x, z), col: 8 (over y, core).
Axes of the slice: x: 4, y: 4, z: 4, core: 2. Of those that a mesh axis runs over, the one named last changes fastest.
Arguments:
- anchor_hidden: bfloat16 [16384, 768], P(('row', 'col')), may hold values from -20 to 20
- candidates: bfloat16 [32768, 768], P(('col', 'row')), may hold values from -8 to 8
- memory: bfloat16 [4, 131072, 768], P(None, ('row', 'col')), may hold values from -6 to 6
- anchor_ids: int32 [16384], P(('row', 'col')), may hold values from 0 to 131071, as said below
- pos_ids: int32 [16384, 4], P(('row', 'col')), may hold values from -1 to 131071, as said below
- pos_count: int32 [16384], P(('row', 'col')), may hold values from 1 to 4
- snapshot: int32 [1], replicated, may hold values from 0 to 2
Outputs:
- loss: float32 [16384], P(('row', 'col'))
- anchor_grad: float32 [16384, 768], P(('row', 'col'))
- cand_grad: float32 [32768, 768], P(('col', 'row'))
The draws below stay inside these ranges and needn't reach their ends.
Inputs may be any that keep to these rules, and one draw needn't show every extreme that they name: `anchor_ids`: node n's memory rows are held by device n // 1024 of row+col. `pos_ids`: slots 0 to pos_count - 1 of a row hold node ids, the others -1. Among the anchor ids and used positive ids of the 128 anchors of one device, at most 12 belong to any one owner device (id // 1024), and exactly 12 to one owner.
All inputs are finite; a program needn't handle non-finite values.
Results may differ from the reference program's by a relative error of at most 0.003.
The reference program's roundings to bfloat16 on the way (of `anchor_row`, `positive`, `query` and `weights`) count: a program that leaves them out, or rounds other values in their place, can miss the bound.
Values may be sent and summed in bfloat16 or wider, within the bound.
No kernel may reach another device: no remote copies, remote signals or barrier semaphores. Data moves between devices by JAX's collectives and lax.ppermute only.
A program may use at most 128 MiB of HBM per device.

```python
import math
import jax
import jax.numpy as jnp
from jax import lax

D = 768
SNAPS = 4
P_MAX = 4
A_DEV = 128
NODE_DEV = 1024
ANCHORS = 16384
CANDS = 32768
NODES = 131072
CAP = 12
N_ROW = 16
N_COL = 8


def request_plan(key):
    devices = N_ROW * N_COL
    slots = 1 + P_MAX
    width = A_DEV * slots
    count_key, order_key, hot_key, other_key, local_key = jax.random.split(key, 5)
    counts = jax.random.randint(count_key, (devices, A_DEV), 1, P_MAX + 1)
    used = jnp.arange(slots)[None, None, :] <= counts[:, :, None]
    used = used.reshape(devices, width)
    orders = jax.vmap(lambda subkey: jax.random.permutation(subkey, width))(jax.random.split(order_key, devices))
    in_order = jnp.take_along_axis(used.astype(jnp.int32), orders, axis=1)
    before = jnp.cumsum(in_order, axis=1) - in_order
    ranks = jax.vmap(lambda places, values: jnp.zeros((width,), jnp.int32).at[places].set(values))(orders, before)
    hottest = jax.random.randint(hot_key, (devices, 1), 0, devices)
    others = jax.vmap(lambda subkey: jax.random.permutation(subkey, devices - 1))(jax.random.split(other_key, devices))
    spread = jnp.take_along_axis(others, jnp.maximum(ranks - CAP, 0) % (devices - 1), axis=1)
    owners = jnp.where(ranks < CAP, hottest, (hottest + 1 + spread) % devices)
    local_rows = jax.random.randint(local_key, (devices, width), 0, NODE_DEV)
    node_list = jnp.where(used, owners * NODE_DEV + local_rows, -1).reshape(ANCHORS, slots)
    return (node_list.astype(jnp.int32), counts.reshape(ANCHORS).astype(jnp.int32))


def drawn_pattern(key):
    return jax.random.uniform(key, (8, D), jnp.float32, -1.7, 1.7)


def score_levels():
    return 110.0 + 190.0 * jnp.arange(8, dtype=jnp.float32) / 7.0


def draw_anchor_ids(key, part):
    node_list, counts = request_plan(key)
    return node_list[:, 0]


def draw_pos_ids(key, part):
    node_list, counts = request_plan(key)
    return node_list[:, 1:]


def draw_pos_count(key, part):
    node_list, counts = request_plan(key)
    return counts


def draw_anchor_hidden(key, part):
    pattern = drawn_pattern(key)
    key = jax.random.fold_in(key, 11)
    base_key = jax.random.fold_in(key, 0)
    base = jax.random.truncated_normal(base_key, -6.0, 6.0, (ANCHORS, D), jnp.float32)
    strength = score_levels() / (0.963 * math.sqrt(D) * 3.5)
    places = jnp.arange(8) * (ANCHORS // 8)
    base = base.at[places].set(pattern * strength[:, None])
    return base.astype(jnp.bfloat16)


def draw_candidates(key, part):
    pattern = drawn_pattern(key)
    key = jax.random.fold_in(key, 12)
    base_key = jax.random.fold_in(key, 0)
    noise_key = jax.random.fold_in(key, 2)
    base = jax.random.truncated_normal(base_key, -6.0, 6.0, (CANDS, D), jnp.float32)
    places = jnp.arange(8) * (CANDS // 8)
    gap = 2.0 / score_levels()
    noise = jax.random.uniform(noise_key, (8, D), jnp.float32, -0.1, 0.1)
    second = 3.5 * (pattern * (1.0 - gap)[:, None] + noise)
    base = base.at[places].set(3.5 * pattern).at[places + 1].set(second)
    return base.astype(jnp.bfloat16)


def steps_of(stream_key, extent, cuts, least, largest):
    def one(position, shards_of):
        draws = jax.random.uniform(jax.random.fold_in(jax.random.fold_in(stream_key, 6), position), (shards_of,), jnp.float32, least / len(cuts), largest / len(cuts))
        return jnp.repeat(jnp.exp(draws), extent[position] // shards_of).reshape((-1,) + (1,) * (len(extent) - position - 1))

    level = one(*cuts[0])
    for cut in cuts[1:]:
        level = level * one(*cut)
    return level


def scatter_about(stream_key, shape, scale, bound, cuts=(), kind=jnp.bfloat16):
    drawn = jax.random.normal(stream_key, shape, jnp.float32) * scale
    if len(cuts) > 0:
        drawn = steps_of(stream_key, shape, cuts, -0.22, 0.18) * drawn
    return jnp.clip(drawn, min=-bound, max=bound).astype(kind)


def setup_inputs(seed: int = 0) -> dict:
    key_of = jax.random.split(jax.random.key(seed), 8)
    return {
        "anchor_hidden": draw_anchor_hidden(jax.random.fold_in(key_of[7], 71), 0),
        "candidates": draw_candidates(jax.random.fold_in(key_of[7], 71), 0),
        "memory": scatter_about(key_of[2], (SNAPS, NODES, D), 1.0, 6.0, ((1, 128),)),
        "anchor_ids": draw_anchor_ids(jax.random.fold_in(key_of[7], 71), 0),
        "pos_ids": draw_pos_ids(jax.random.fold_in(key_of[7], 71), 0),
        "pos_count": draw_pos_count(jax.random.fold_in(key_of[7], 71), 0),
        "snapshot": jax.random.randint(key_of[6], (1,), 0, SNAPS - 1).astype(jnp.int32),
    }


def reference(anchor_hidden, candidates, memory, anchor_ids, pos_ids, pos_count, snapshot):
    scale = 1.0 / (D ** 0.5)
    first = snapshot[0]
    current = lax.dynamic_index_in_dim(memory, first, 0, keepdims=False)
    following = lax.dynamic_index_in_dim(memory, first + 1, 0, keepdims=False)
    anchor_row = jnp.take(current, anchor_ids, axis=0)
    summed = jnp.zeros((ANCHORS, D), jnp.float32)
    for column in range(P_MAX):
        listed = pos_ids[:, column]
        fetched = jnp.take(following, jnp.maximum(listed, 0), axis=0).astype(jnp.float32)
        summed = summed + jnp.where((listed >= 0)[:, None], fetched, jnp.zeros((), jnp.float32))
    positive = (summed / pos_count.astype(jnp.float32)[:, None]).astype(jnp.bfloat16)
    query = (anchor_hidden.astype(jnp.float32) + anchor_row.astype(jnp.float32)).astype(jnp.bfloat16)
    block_rows = A_DEV * N_COL
    groups = ANCHORS // block_rows

    def one_block(carry, inputs):
        rows, pos_rows = inputs
        logits = jnp.dot(rows, candidates.T, preferred_element_type=jnp.float32) * scale
        pos_logit = jnp.sum(rows.astype(jnp.float32) * pos_rows.astype(jnp.float32), axis=1) * scale
        top_value = jnp.max(logits, axis=1)
        exp_total = jnp.sum(jnp.exp(logits - top_value[:, None]), axis=1)
        log_total = top_value + jnp.log(exp_total + jnp.exp(pos_logit - top_value))
        weights = jnp.exp(logits - log_total[:, None]).astype(jnp.bfloat16)
        own_grad = jnp.dot(weights, candidates, preferred_element_type=jnp.float32)
        own_grad = own_grad + (jnp.exp(pos_logit - log_total) - 1.0)[:, None] * pos_rows.astype(jnp.float32)
        carry = carry + jnp.dot(weights.T, rows, preferred_element_type=jnp.float32)
        return carry, (log_total - pos_logit, own_grad)

    start = jnp.zeros((CANDS, D), jnp.float32)
    cand_grad, (losses, grads) = lax.scan(
        one_block, start,
        (query.reshape(groups, block_rows, D), positive.reshape(groups, block_rows, D)))
    return losses.reshape(ANCHORS), grads.reshape(ANCHORS, D), cand_grad
```

```python
import functools
import math

import jax
import jax.numpy as jnp
from jax import lax
from jax.experimental import pallas as pl
from jax.experimental.pallas import tpu as pltpu
from jax.sharding import PartitionSpec as P

BF = jnp.bfloat16
F32 = jnp.float32
I32 = jnp.int32
SIDE = 4
VMEM_BYTES = 48 * 1024 * 1024
MAIN = 8
SPARE = 4
TILE = 256


def params(**extra):
    return pltpu.CompilerParams(vmem_limit_bytes=VMEM_BYTES, **extra)


def cost(flops, moved, exps=0):
    return pl.CostEstimate(flops=flops, bytes_accessed=moved, transcendentals=exps)


def nn(a, b):
    return jnp.dot(a, b, preferred_element_type=F32)


def shift_x(value, by):
    pairs = [(x * SIDE + z, (x + by) % SIDE * SIDE + z) for x in range(SIDE) for z in range(SIDE)]
    return lax.ppermute(value, "row", pairs)


def shift_z(value, by):
    pairs = [(x * SIDE + z, x * SIDE + (z + by) % SIDE) for x in range(SIDE) for z in range(SIDE)]
    return lax.ppermute(value, "row", pairs)


def shift_y(value, by):
    pairs = [(y * 2 + k, (y + by) % SIDE * 2 + k) for y in range(SIDE) for k in range(2)]
    return lax.ppermute(value, "col", pairs)


def swap_core(value):
    return lax.ppermute(value, "col", [(i, i ^ 1) for i in range(2 * SIDE)])


def plan_kernel(rows_ref, cols_ref, request_ref, place_ref):
    rows, cols = rows_ref[...], cols_ref[...]
    kinds, anchors = rows.shape
    total = kinds * anchors
    across = jnp.concatenate([rows[k : k + 1, :] for k in range(kinds)], axis=1)
    down = jnp.concatenate([cols[:, k : k + 1] for k in range(kinds)], axis=0)
    owner_across = jnp.where(across >= 0, across >> 10, -1)
    owner_down = jnp.where(down >= 0, down >> 10, -2)
    first = lax.broadcasted_iota(I32, (total, total), 0)
    second = lax.broadcasted_iota(I32, (total, total), 1)
    same = (owner_down == owner_across) & (second < first)
    slot = jnp.sum(jnp.where(same, 1.0, 0.0), axis=1, keepdims=True).astype(I32)
    kind = jnp.where(lax.broadcasted_iota(I32, (total, 1), 0) < anchors, 0, 1024)
    code = (down & 1023) + kind + 1
    hit = (slot == lax.broadcasted_iota(I32, (total, 128), 1)) & (down >= 0)
    low = jnp.where(hit, code & 63, 0).astype(F32).astype(BF)
    high = jnp.where(hit, code >> 6, 0).astype(F32).astype(BF)
    devices = request_ref.shape[0]
    pick = jnp.where(owner_across == lax.broadcasted_iota(I32, (devices, total), 0), 1.0, 0.0).astype(BF)
    found = nn(pick, low) + 64.0 * nn(pick, high) - 1.0
    request_ref[...] = found[:, : request_ref.shape[1]].astype(I32)
    place = jnp.where(down >= 0, owner_down * 16 + slot, -1)
    for k in range(kinds):
        place_ref[:, k : k + 1] = place[k * anchors : (k + 1) * anchors]


def plan(rows, cols):
    return pl.pallas_call(
        plan_kernel,
        out_shape=(jax.ShapeDtypeStruct((128, 16), I32), jax.ShapeDtypeStruct(cols.shape, I32)),
        compiler_params=params(),
        name="plan",
    )(rows, cols)


def serve_kernel(snap_ref, asked_ref, current_ref, following_ref, out_ref):
    asked = asked_ref[...]
    devices, lanes = asked.shape
    count = devices * MAIN
    wide = jnp.broadcast_to(asked[:, None, :], (devices, MAIN, lanes)).reshape(count, lanes)
    lane = lax.broadcasted_iota(I32, (count, lanes), 1)
    spot = lax.broadcasted_iota(I32, (count, lanes), 0) & (MAIN - 1)
    main = jnp.sum(jnp.where(lane == spot, wide, 0), axis=1, keepdims=True)
    spare = jnp.sum(jnp.where(lane == MAIN + (spot & (SPARE - 1)), wide, 0), axis=1, keepdims=True)
    nodes, width = current_ref.shape[1:]
    node = lax.broadcasted_iota(I32, (count, nodes), 1)

    def rows_of(code):
        now = jnp.where(node == code, 1.0, 0.0).astype(BF)
        later = jnp.where(node + nodes == code, 1.0, 0.0).astype(BF)
        return (nn(now, current_ref[0]) + nn(later, following_ref[0])).astype(BF)

    out_ref[:, :width] = rows_of(main)
    extra = rows_of(spare)
    half = width // 2
    upper = (lax.broadcasted_iota(I32, (count, half), 0) & (MAIN - 1)) < SPARE
    out_ref[:, width:] = jnp.where(upper, extra[:, :half].astype(F32), extra[:, half:].astype(F32)).astype(BF)


def serve(snapshot, asked, memory):
    devices, lanes = asked.shape
    _, nodes, width = memory.shape
    step = 32
    return pl.pallas_call(
        serve_kernel,
        grid_spec=pltpu.PrefetchScalarGridSpec(
            num_scalar_prefetch=1,
            grid=(devices // step,),
            in_specs=[
                pl.BlockSpec((step, lanes), lambda i, s: (i, 0)),
                pl.BlockSpec((1, nodes, width), lambda i, s: (s[0], 0, 0)),
                pl.BlockSpec((1, nodes, width), lambda i, s: (s[0] + 1, 0, 0)),
            ],
            out_specs=pl.BlockSpec((step * MAIN, width + width // 2), lambda i, s: (i, 0)),
        ),
        out_shape=jax.ShapeDtypeStruct((devices * MAIN, width + width // 2), BF),
        compiler_params=params(),
        name="serve",
    )(snapshot, asked, memory, memory)


def unpack_kernel(scale, got_ref, place_ref, hidden_ref, count_ref, query_ref, positive_ref, logit_ref):
    anchors, kinds = place_ref.shape
    total, wide = got_ref.shape
    width = hidden_ref.shape[1]
    spot = lax.broadcasted_iota(I32, (anchors, total), 1)

    def masks(k):
        place = place_ref[:, k : k + 1]
        base, slot = (place >> 4) * MAIN, place & 15
        live = place >= 0
        main = jnp.where(live & (slot < MAIN), base + slot, -1)
        upper = jnp.where(live & (slot >= MAIN), base + slot - MAIN, -1)
        lower = jnp.where(live & (slot >= MAIN), base + slot - MAIN + SPARE, -1)
        return [jnp.where(spot == at, 1.0, 0.0) for at in (main, upper, lower)]

    first = masks(0)
    others = masks(1)
    for k in range(2, kinds):
        others = [a + b for a, b in zip(others, masks(k))]
    picks = [jnp.concatenate([a, b], axis=0).astype(BF) for a, b in zip(first, others)]
    rows = nn(picks[0], got_ref[:, :width])
    tail = got_ref[:, width:]
    rows = rows + jnp.concatenate([nn(picks[1], tail), nn(picks[2], tail)], axis=1)
    query = (hidden_ref[...].astype(F32) + rows[:anchors]).astype(BF)
    positive = (rows[anchors:] / count_ref[...].astype(F32)).astype(BF)
    query_ref[...] = query
    positive_ref[...] = positive
    logit_ref[...] = jnp.sum(query.astype(F32) * positive.astype(F32), axis=1, keepdims=True) * scale


def unpack(got, place, hidden, count, scale):
    anchors, width = hidden.shape
    return pl.pallas_call(
        functools.partial(unpack_kernel, scale),
        out_shape=(
            jax.ShapeDtypeStruct((anchors, width), BF),
            jax.ShapeDtypeStruct((anchors, width), BF),
            jax.ShapeDtypeStruct((anchors, 1), F32),
        ),
        compiler_params=params(),
        name="unpack",
    )(got, place, hidden, count)


def score_kernel(scale, cand_ref, query_ref, logit_ref, level_ref):
    logits = lax.dot_general(cand_ref[...], query_ref[...], (((1,), (1,)), ((), ())), preferred_element_type=F32) * scale
    logit_ref[...] = logits
    top = jnp.max(logits, axis=0, keepdims=True)
    level_ref[0] = top + jnp.log(jnp.sum(jnp.exp(logits - top), axis=0, keepdims=True))


def score(cands, queries, scale):
    cand_count, width = cands.shape
    anchors = queries.shape[0]
    steps = anchors // TILE
    return pl.pallas_call(
        functools.partial(score_kernel, scale),
        grid=(steps,),
        in_specs=[
            pl.BlockSpec((cand_count, width), lambda i: (0, 0)),
            pl.BlockSpec((TILE, width), lambda i: (i, 0)),
        ],
        out_specs=(
            pl.BlockSpec((cand_count, TILE), lambda i: (0, i)),
            pl.BlockSpec((1, 1, TILE), lambda i: (i, 0, 0)),
        ),
        out_shape=(
            jax.ShapeDtypeStruct((cand_count, anchors), F32),
            jax.ShapeDtypeStruct((steps, 1, TILE), F32),
        ),
        compiler_params=params(),
        cost_estimate=cost(2 * cand_count * anchors * width, 4 * cand_count * anchors, cand_count * anchors),
        name="score",
    )(cands, queries)


def anchor_kernel(logit_ref, level_ref, turned_ref, part_ref):
    weights = jnp.exp(logit_ref[...] - level_ref[0]).astype(BF)
    part_ref[...] = nn(turned_ref[...], weights)


def anchor_terms(logits, level, turned):
    cand_count, anchors = logits.shape
    width = turned.shape[0]
    return pl.pallas_call(
        anchor_kernel,
        grid=(anchors // TILE,),
        in_specs=[
            pl.BlockSpec((cand_count, TILE), lambda i: (0, i)),
            pl.BlockSpec((1, 1, TILE), lambda i: (i, 0, 0)),
            pl.BlockSpec((width, cand_count), lambda i: (0, 0)),
        ],
        out_specs=pl.BlockSpec((width, TILE), lambda i: (0, i)),
        out_shape=jax.ShapeDtypeStruct((width, anchors), F32),
        compiler_params=params(),
        cost_estimate=cost(2 * cand_count * anchors * width, 4 * cand_count * anchors, cand_count * anchors),
        name="anchor_terms",
    )(logits, level, turned)


def cand_kernel(logit_ref, total_ref, query_ref, part_ref):
    weights = jnp.exp(logit_ref[...] - total_ref[...]).astype(BF)
    part_ref[...] = nn(weights, query_ref[...]).astype(part_ref.dtype)


def cand_terms(logits, total, queries, first, count, kind):
    anchors, width = queries.shape
    start = first // TILE
    return pl.pallas_call(
        cand_kernel,
        grid=(count // TILE,),
        in_specs=[
            pl.BlockSpec((TILE, anchors), lambda i: (i + start, 0)),
            pl.BlockSpec((1, anchors), lambda i: (0, 0)),
            pl.BlockSpec((anchors, width), lambda i: (0, 0)),
        ],
        out_specs=pl.BlockSpec((TILE, width), lambda i: (i, 0)),
        out_shape=jax.ShapeDtypeStruct((count, width), kind),
        compiler_params=params(),
        cost_estimate=cost(2 * count * anchors * width, 4 * count * anchors, count * anchors),
        name="cand_terms",
    )(logits, total, queries)


def merge(levels):
    top = functools.reduce(jnp.maximum, levels)
    return top + jnp.log(sum(jnp.exp(level - top) for level in levels))


def body(anchor_hidden, candidates, memory, anchor_ids, pos_ids, pos_count, snapshot):
    anchors, width = anchor_hidden.shape
    scale = 1.0 / math.sqrt(width)
    half = width // 2

    along_y = jnp.concatenate([candidates] + [shift_y(candidates, d) for d in (1, 2, 3)], axis=0)
    cands = jnp.concatenate([along_y, swap_core(along_y)], axis=0)
    turned = cands.T

    ids = jnp.concatenate([anchor_ids[:, None], pos_ids], axis=1)
    requests, place = plan(ids.T, ids)
    asked = lax.all_to_all(requests, ("row", "col"), split_axis=0, concat_axis=0, tiled=True)
    served = serve(snapshot, asked, memory)
    devices = asked.shape[0]
    served = served.reshape(devices, MAIN, width + half)
    got = lax.all_to_all(served, ("row", "col"), split_axis=0, concat_axis=0, tiled=True)
    got = got.reshape(devices * MAIN, width + half)
    query, positive, pos_logit = unpack(got, place, anchor_hidden, pos_count[:, None], scale)
    pos_logit = pos_logit.reshape(anchors)

    left, right = query[:, :half], query[:, half:]
    left = jnp.stack([left] + [shift_z(left, d) for d in (1, 2, 3)])
    right = jnp.stack([right] + [shift_x(right, d) for d in (1, 2, 3)])
    left = jnp.stack([left] + [shift_x(left, d) for d in (1, 2, 3)])
    right = jnp.stack([right] + [shift_z(right, d) for d in (1, 2, 3)], axis=1)
    queries = jnp.concatenate([left, right], axis=3).reshape(SIDE * SIDE * anchors, width)

    logits, level = score(cands, queries, scale)
    parts = anchor_terms(logits, level, turned)

    known = level.reshape(SIDE * SIDE, anchors)
    own = merge([known[0], pos_logit])
    known = jnp.concatenate([own[None], known[1:]], axis=0).reshape(SIDE, SIDE, anchors)
    known = merge([known] + [jnp.roll(shift_z(known, d), d, axis=1) for d in (1, 2, 3)])
    known = merge([known] + [jnp.roll(shift_x(known, d), d, axis=0) for d in (1, 2, 3)])
    log_total = known[0, 0]
    total = known.reshape(1, SIDE * SIDE * anchors)

    count = cands.shape[0] // 2
    away = cand_terms(logits, total, queries, count, count, BF)
    came = swap_core(away).astype(F32)
    home = cand_terms(logits, total, queries, 0, count, F32)
    shard = candidates.shape[0]
    held = [home[d * shard : (d + 1) * shard] + came[d * shard : (d + 1) * shard] for d in range(SIDE)]
    cand_grad = held[0]
    for d in (1, 2, 3):
        cand_grad = cand_grad + shift_y(held[d].astype(BF), -d).astype(F32)

    factor = jnp.exp(level.reshape(1, -1) - total)
    scaled = (parts * factor).reshape(width, SIDE, SIDE, anchors)
    upper, lower = scaled[:half], scaled[half:]
    upper_sum = upper[:, 0]
    lower_sum = lower[:, :, 0]
    for d in (1, 2, 3):
        upper_sum = upper_sum + shift_x(upper[:, d].reshape(half, -1).astype(BF), -d).astype(F32).reshape(half, SIDE, anchors)
        lower_sum = lower_sum + shift_z(lower[:, :, d].reshape(half, -1).astype(BF), -d).astype(F32).reshape(half, SIDE, anchors)
    upper_all, lower_all = upper_sum[:, 0], lower_sum[:, 0]
    for d in (1, 2, 3):
        upper_all = upper_all + shift_z(upper_sum[:, d].astype(BF), -d).astype(F32)
        lower_all = lower_all + shift_x(lower_sum[:, d].astype(BF), -d).astype(F32)
    weighted = jnp.concatenate([upper_all, lower_all], axis=0).T

    anchor_grad = weighted + (jnp.exp(pos_logit - log_total) - 1.0)[:, None] * positive.astype(F32)
    loss = log_total - pos_logit
    return (loss, anchor_grad, cand_grad)


def solution(mesh):
    in_specs = (
        P(("row", "col"), None),
        P(("col", "row"), None),
        P(None, ("row", "col"), None),
        P(("row", "col")),
        P(("row", "col"), None),
        P(("row", "col")),
        P(),
    )
    out_specs = (P(("row", "col")), P(("row", "col"), None), P(("col", "row"), None))
    return jax.shard_map(body, mesh=mesh, in_specs=in_specs, out_specs=out_specs, check_vma=False)
```

```python
import functools
import math

import jax
import jax.numpy as jnp
from jax import lax
from jax.experimental import pallas as pl
from jax.experimental.pallas import tpu as pltpu
from jax.sharding import PartitionSpec as P

BF = jnp.bfloat16
F32 = jnp.float32
I32 = jnp.int32
SIDE = 4
VMEM_BYTES = 40 * 1024 * 1024
MAIN = 8
SPARE = 4
TILE = 512


def params(**extra):
    return pltpu.CompilerParams(vmem_limit_bytes=VMEM_BYTES, **extra)


def cost(flops, moved, exps=0):
    return pl.CostEstimate(flops=flops, bytes_accessed=moved, transcendentals=exps)


def nn(a, b):
    return jnp.dot(a, b, preferred_element_type=F32)


def shift_x(value, by):
    pairs = [(x * SIDE + z, (x + by) % SIDE * SIDE + z) for x in range(SIDE) for z in range(SIDE)]
    return lax.ppermute(value, "row", pairs)


def shift_z(value, by):
    pairs = [(x * SIDE + z, x * SIDE + (z + by) % SIDE) for x in range(SIDE) for z in range(SIDE)]
    return lax.ppermute(value, "row", pairs)


def shift_y(value, by):
    pairs = [(y * 2 + k, (y + by) % SIDE * 2 + k) for y in range(SIDE) for k in range(2)]
    return lax.ppermute(value, "col", pairs)


def swap_core(value):
    return lax.ppermute(value, "col", [(i, i ^ 1) for i in range(2 * SIDE)])


def plan_kernel(rows_ref, cols_ref, request_ref, place_ref):
    rows, cols = rows_ref[...], cols_ref[...]
    kinds, anchors = rows.shape
    total = kinds * anchors
    across = jnp.concatenate([rows[k : k + 1, :] for k in range(kinds)], axis=1)
    down = jnp.concatenate([cols[:, k : k + 1] for k in range(kinds)], axis=0)
    owner_across = jnp.where(across >= 0, across >> 10, -1)
    owner_down = jnp.where(down >= 0, down >> 10, -2)
    first = lax.broadcasted_iota(I32, (total, total), 0)
    second = lax.broadcasted_iota(I32, (total, total), 1)
    same = (owner_down == owner_across) & (second < first)
    slot = jnp.sum(jnp.where(same, 1.0, 0.0), axis=1, keepdims=True).astype(I32)
    kind = jnp.where(lax.broadcasted_iota(I32, (total, 1), 0) < anchors, 0, 1024)
    code = (down & 1023) + kind + 1
    hit = (slot == lax.broadcasted_iota(I32, (total, 128), 1)) & (down >= 0)
    low = jnp.where(hit, code & 63, 0).astype(F32).astype(BF)
    high = jnp.where(hit, code >> 6, 0).astype(F32).astype(BF)
    devices = request_ref.shape[0]
    pick = jnp.where(owner_across == lax.broadcasted_iota(I32, (devices, total), 0), 1.0, 0.0).astype(BF)
    found = nn(pick, low) + 64.0 * nn(pick, high) - 1.0
    request_ref[...] = found[:, : request_ref.shape[1]].astype(I32)
    place = jnp.where(down >= 0, owner_down * 16 + slot, -1)
    for k in range(kinds):
        place_ref[:, k : k + 1] = place[k * anchors : (k + 1) * anchors]


def plan(rows, cols):
    return pl.pallas_call(
        plan_kernel,
        out_shape=(jax.ShapeDtypeStruct((128, 16), I32), jax.ShapeDtypeStruct(cols.shape, I32)),
        compiler_params=params(),
        name="plan",
    )(rows, cols)


def serve_kernel(snap_ref, asked_ref, current_ref, following_ref, out_ref):
    asked = asked_ref[...]
    devices, lanes = asked.shape
    count = devices * MAIN
    wide = jnp.broadcast_to(asked[:, None, :], (devices, MAIN, lanes)).reshape(count, lanes)
    lane = lax.broadcasted_iota(I32, (count, lanes), 1)
    spot = lax.broadcasted_iota(I32, (count, lanes), 0) & (MAIN - 1)
    main = jnp.sum(jnp.where(lane == spot, wide, 0), axis=1, keepdims=True)
    spare = jnp.sum(jnp.where(lane == MAIN + (spot & (SPARE - 1)), wide, 0), axis=1, keepdims=True)
    nodes, width = current_ref.shape[1:]
    node = lax.broadcasted_iota(I32, (count, nodes), 1)

    def rows_of(code):
        now = jnp.where(node == code, 1.0, 0.0).astype(BF)
        later = jnp.where(node + nodes == code, 1.0, 0.0).astype(BF)
        return (nn(now, current_ref[0]) + nn(later, following_ref[0])).astype(BF)

    out_ref[:, :width] = rows_of(main)
    extra = rows_of(spare)
    half = width // 2
    upper = (lax.broadcasted_iota(I32, (count, half), 0) & (MAIN - 1)) < SPARE
    out_ref[:, width:] = jnp.where(upper, extra[:, :half].astype(F32), extra[:, half:].astype(F32)).astype(BF)


def serve(snapshot, asked, memory):
    devices, lanes = asked.shape
    _, nodes, width = memory.shape
    step = 32
    return pl.pallas_call(
        serve_kernel,
        grid_spec=pltpu.PrefetchScalarGridSpec(
            num_scalar_prefetch=1,
            grid=(devices // step,),
            in_specs=[
                pl.BlockSpec((step, lanes), lambda i, s: (i, 0)),
                pl.BlockSpec((1, nodes, width), lambda i, s: (s[0], 0, 0)),
                pl.BlockSpec((1, nodes, width), lambda i, s: (s[0] + 1, 0, 0)),
            ],
            out_specs=pl.BlockSpec((step * MAIN, width + width // 2), lambda i, s: (i, 0)),
        ),
        out_shape=jax.ShapeDtypeStruct((devices * MAIN, width + width // 2), BF),
        compiler_params=params(),
        name="serve",
    )(snapshot, asked, memory, memory)


def unpack_kernel(scale, got_ref, place_ref, hidden_ref, count_ref, query_ref, positive_ref, logit_ref):
    anchors, kinds = place_ref.shape
    total, wide = got_ref.shape
    width = hidden_ref.shape[1]
    spot = lax.broadcasted_iota(I32, (anchors, total), 1)

    def masks(k):
        place = place_ref[:, k : k + 1]
        base, slot = (place >> 4) * MAIN, place & 15
        live = place >= 0
        main = jnp.where(live & (slot < MAIN), base + slot, -1)
        upper = jnp.where(live & (slot >= MAIN), base + slot - MAIN, -1)
        lower = jnp.where(live & (slot >= MAIN), base + slot - MAIN + SPARE, -1)
        return [jnp.where(spot == at, 1.0, 0.0) for at in (main, upper, lower)]

    first = masks(0)
    others = masks(1)
    for k in range(2, kinds):
        others = [a + b for a, b in zip(others, masks(k))]
    picks = [jnp.concatenate([a, b], axis=0).astype(BF) for a, b in zip(first, others)]
    rows = nn(picks[0], got_ref[:, :width])
    tail = got_ref[:, width:]
    rows = rows + jnp.concatenate([nn(picks[1], tail), nn(picks[2], tail)], axis=1)
    query = (hidden_ref[...].astype(F32) + rows[:anchors]).astype(BF)
    positive = (rows[anchors:] / count_ref[...].astype(F32)).astype(BF)
    query_ref[...] = query
    positive_ref[...] = positive
    logit_ref[...] = jnp.sum(query.astype(F32) * positive.astype(F32), axis=1, keepdims=True) * scale


def unpack(got, place, hidden, count, scale):
    anchors, width = hidden.shape
    return pl.pallas_call(
        functools.partial(unpack_kernel, scale),
        out_shape=(
            jax.ShapeDtypeStruct((anchors, width), BF),
            jax.ShapeDtypeStruct((anchors, width), BF),
            jax.ShapeDtypeStruct((anchors, 1), F32),
        ),
        compiler_params=params(),
        name="unpack",
    )(got, place, hidden, count)


def score_kernel(unit, cand_ref, query_ref, logit_ref, top_ref, level_ref, part_ref):
    cands = cand_ref[...]
    logits = lax.dot_general(cands, query_ref[...], (((1,), (1,)), ((), ())), preferred_element_type=F32)
    logit_ref[...] = logits
    top = jnp.max(logits, axis=0, keepdims=True) * unit
    weights = jnp.exp2(logits * unit - top)
    top_ref[...] = top
    level_ref[...] = top + jnp.log2(jnp.sum(weights, axis=0, keepdims=True))
    part = lax.dot_general(weights.astype(BF), cands, (((0,), (0,)), ((), ())), preferred_element_type=F32)
    part_ref[...] = part


def score(cands, queries, unit):
    cand_count, width = cands.shape
    anchors = queries.shape[0]
    pairs = cand_count * anchors
    return pl.pallas_call(
        functools.partial(score_kernel, unit),
        out_shape=(
            jax.ShapeDtypeStruct((cand_count, anchors), F32),
            jax.ShapeDtypeStruct((1, anchors), F32),
            jax.ShapeDtypeStruct((1, anchors), F32),
            jax.ShapeDtypeStruct((anchors, width), F32),
        ),
        compiler_params=params(),
        cost_estimate=cost(4 * pairs * width, 4 * pairs, pairs),
        name="score",
    )(cands, queries)


def cand_kernel(unit, *refs):
    logit_refs, (total_ref, query_ref, part_ref) = refs[:-3], refs[-3:]
    weights, start = [], 0
    for ref in logit_refs:
        stop = start + ref.shape[1]
        weights.append(jnp.exp2(ref[...] * unit - total_ref[:, start:stop]).astype(BF))
        start = stop
    part_ref[...] = nn(jnp.concatenate(weights, axis=1), query_ref[...]).astype(part_ref.dtype)


def cand_terms(logits, total, queries, first, count, kind, unit):
    anchors, width = queries.shape
    start = first // TILE
    pairs = count * anchors
    return pl.pallas_call(
        functools.partial(cand_kernel, unit),
        grid=(count // TILE,),
        in_specs=[pl.BlockSpec((TILE, part.shape[1]), lambda i: (i + start, 0)) for part in logits]
        + [
            pl.BlockSpec((1, anchors), lambda i: (0, 0)),
            pl.BlockSpec((anchors, width), lambda i: (0, 0)),
        ],
        out_specs=pl.BlockSpec((TILE, width), lambda i: (i, 0)),
        out_shape=jax.ShapeDtypeStruct((count, width), kind),
        compiler_params=params(),
        cost_estimate=cost(2 * pairs * width, 4 * pairs, pairs),
        name="cand_terms",
    )(*logits, total, queries)


def merge(levels):
    top = functools.reduce(jnp.maximum, levels)
    return top + jnp.log2(sum(jnp.exp2(level - top) for level in levels))


def table_kernel(*refs):
    level_refs, (logit_ref, table_ref) = refs[:-2], refs[-2:]
    half = table_ref.shape[1] // 2
    rows = []
    for x in range(SIDE):
        for z in range(SIDE):
            a_part = level_refs[x][:, z * half : (z + 1) * half]
            b_part = level_refs[z][:, (SIDE + x) * half : (SIDE + x + 1) * half]
            rows.append(jnp.concatenate([a_part, b_part], axis=1))
    rows[0] = merge([rows[0], logit_ref[...] * math.log2(math.e)])
    table_ref[...] = jnp.concatenate(rows, axis=0)


def table(levels, pos_logit, anchors):
    return pl.pallas_call(
        table_kernel,
        out_shape=jax.ShapeDtypeStruct((SIDE * SIDE, anchors), F32),
        compiler_params=params(),
        name="level_table",
    )(*levels, pos_logit)


def rolled(value, along_x, by):
    if along_x:
        cut = (SIDE - by) * SIDE
        return jnp.concatenate([value[cut:], value[:cut]], axis=0)
    rows = []
    for x in range(SIDE):
        cut = x * SIDE + SIDE - by
        rows += [value[cut : (x + 1) * SIDE], value[x * SIDE : cut]]
    return jnp.concatenate(rows, axis=0)


def merge_kernel(along_x, own_ref, *refs):
    came_refs, out_ref = refs[:-1], refs[-1]
    levels = [own_ref[...]]
    for by, ref in zip((1, 2, 3), came_refs):
        levels.append(rolled(ref[...], along_x, by))
    out_ref[...] = merge(levels)


def merged(own, came, along_x):
    return pl.pallas_call(
        functools.partial(merge_kernel, along_x),
        out_shape=jax.ShapeDtypeStruct(own.shape, F32),
        compiler_params=params(),
        name="level_merge",
    )(own, *came)


def spread_kernel(own_ref, *refs):
    came_refs, top_refs, (total_ref, factor_ref, log_ref) = refs[:3], refs[3:7], refs[7:]
    levels = [own_ref[...]]
    for by, ref in zip((1, 2, 3), came_refs):
        levels.append(rolled(ref[...], True, by))
    table = merge(levels)
    half = table.shape[1] // 2
    for j in range(SIDE):
        a_parts = [table[j * SIDE + i : j * SIDE + i + 1, :half] for i in range(SIDE)]
        b_parts = [table[i * SIDE + j : i * SIDE + j + 1, half:] for i in range(SIDE)]
        row = jnp.concatenate(a_parts + b_parts, axis=1)
        size = row.shape[1]
        total_ref[:, j * size : (j + 1) * size] = row
        factor_ref[:, j * size : (j + 1) * size] = jnp.exp2(top_refs[j][...] - row)
    log_ref[...] = table[0:1] * math.log(2.0)


def spread(own, came, tops):
    groups, anchors = own.shape
    return pl.pallas_call(
        spread_kernel,
        out_shape=(
            jax.ShapeDtypeStruct((1, groups * anchors), F32),
            jax.ShapeDtypeStruct((1, groups * anchors), F32),
            jax.ShapeDtypeStruct((1, anchors), F32),
        ),
        compiler_params=params(),
        name="level_spread",
    )(own, *came, *tops)


def body(anchor_hidden, candidates, memory, anchor_ids, pos_ids, pos_count, snapshot):
    anchors, width = anchor_hidden.shape
    scale = 1.0 / math.sqrt(width)
    unit = scale * math.log2(math.e)
    half = anchors // 2
    steps = (1, 2, 3)

    along_y = jnp.concatenate([candidates] + [shift_y(candidates, d) for d in steps], axis=0)
    cands = jnp.concatenate([along_y, swap_core(along_y)], axis=0)

    ids = jnp.concatenate([anchor_ids[:, None], pos_ids], axis=1)
    requests, place = plan(ids.T, ids)
    asked = lax.all_to_all(requests, ("row", "col"), split_axis=0, concat_axis=0, tiled=True)
    served = serve(snapshot, asked, memory)
    served, cands = lax.optimization_barrier((served, cands))
    devices = asked.shape[0]
    served = served.reshape(devices, MAIN, served.shape[1])
    got = lax.all_to_all(served, ("row", "col"), split_axis=0, concat_axis=0, tiled=True)
    got = got.reshape(devices * MAIN, got.shape[2])
    query, positive, pos_logit = unpack(got, place, anchor_hidden, pos_count[:, None], scale)
    pos_logit = pos_logit.reshape(anchors)

    first, second = query[:half], query[half:]
    first = jnp.concatenate([first] + [shift_z(first, d) for d in steps], axis=0)
    second = jnp.concatenate([second] + [shift_x(second, d) for d in steps], axis=0)
    groups = [jnp.concatenate([first, second], axis=0)]
    for d in (1, 3, 2):
        groups.append(jnp.concatenate([shift_x(first, d), shift_z(second, d)], axis=0))
    groups = [groups[0], groups[1], groups[3], groups[2]]
    scored = [score(cands, group, unit) for group in groups]
    logits = [one[0] for one in scored]
    tops = [one[1] for one in scored]
    levels = [one[2] for one in scored]
    parts = [one[3] for one in scored]

    known = table(levels, pos_logit.reshape(1, anchors), anchors)
    known = merged(known, [shift_z(known, d) for d in steps], False)
    total, factor, log_total = spread(known, [shift_x(known, d) for d in steps], tops)
    log_total = log_total.reshape(anchors)
    factors = factor.reshape(SIDE, -1)

    queries = jnp.concatenate(groups, axis=0)
    count = cands.shape[0] // 2
    away = cand_terms(logits, total, queries, count, count, BF, unit)
    came = swap_core(away).astype(F32)

    size = SIDE * half
    scaled = [part * factors[j][:, None] for j, part in enumerate(parts)]
    a_sum, b_sum = scaled[0][:size], scaled[0][size:]
    for d in steps:
        sent = scaled[d].astype(BF)
        a_sum = a_sum + shift_x(sent[:size], -d).astype(F32)
        b_sum = b_sum + shift_z(sent[size:], -d).astype(F32)
    a_all, b_all = a_sum[:half], b_sum[:half]
    for d in steps:
        a_all = a_all + shift_z(a_sum[d * half : (d + 1) * half].astype(BF), -d).astype(F32)
        b_all = b_all + shift_x(b_sum[d * half : (d + 1) * half].astype(BF), -d).astype(F32)
    weighted = jnp.concatenate([a_all, b_all], axis=0)
    anchor_grad = weighted + (jnp.exp(pos_logit - log_total) - 1.0)[:, None] * positive.astype(F32)
    loss = log_total - pos_logit

    home = cand_terms(logits, total, queries, 0, count, F32, unit)
    shard = candidates.shape[0]
    held = [home[d * shard : (d + 1) * shard] + came[d * shard : (d + 1) * shard] for d in range(SIDE)]
    cand_grad = held[0]
    for d in steps:
        cand_grad = cand_grad + shift_y(held[d].astype(BF), -d).astype(F32)
    return (loss, anchor_grad, cand_grad)


def solution(mesh):
    in_specs = (
        P(("row", "col"), None),
        P(("col", "row"), None),
        P(None, ("row", "col"), None),
        P(("row", "col")),
        P(("row", "col"), None),
        P(("row", "col")),
        P(),
    )
    out_specs = (P(("row", "col")), P(("row", "col"), None), P(("col", "row"), None))
    return jax.shard_map(body, mesh=mesh, in_specs=in_specs, out_specs=out_specs, check_vma=False)
```

```python
import functools
import math

import jax
import jax.numpy as jnp
from jax import lax
from jax.experimental import pallas as pl
from jax.experimental.pallas import tpu as pltpu
from jax.sharding import PartitionSpec as P

BF = jnp.bfloat16
F32 = jnp.float32
I32 = jnp.int32
SIDE = 4
MIB = 1024 * 1024
MAIN = 8
SPARE = 4
TILE = 512


def params(mib):
    return pltpu.CompilerParams(vmem_limit_bytes=mib * MIB)


def cost(flops, moved, exps=0):
    return pl.CostEstimate(flops=flops, bytes_accessed=moved, transcendentals=exps)


def nn(a, b):
    return jnp.dot(a, b, preferred_element_type=F32)


def shift_x(value, by):
    pairs = [(x * SIDE + z, (x + by) % SIDE * SIDE + z) for x in range(SIDE) for z in range(SIDE)]
    return lax.ppermute(value, "row", pairs)


def shift_z(value, by):
    pairs = [(x * SIDE + z, x * SIDE + (z + by) % SIDE) for x in range(SIDE) for z in range(SIDE)]
    return lax.ppermute(value, "row", pairs)


def shift_y(value, by):
    pairs = [(y * 2 + k, (y + by) % SIDE * 2 + k) for y in range(SIDE) for k in range(2)]
    return lax.ppermute(value, "col", pairs)


def swap_core(value):
    return lax.ppermute(value, "col", [(i, i ^ 1) for i in range(2 * SIDE)])


def plan_kernel(rows_ref, cols_ref, request_ref, place_ref):
    rows, cols = rows_ref[...], cols_ref[...]
    kinds, anchors = rows.shape
    total = kinds * anchors
    across = jnp.concatenate([rows[k : k + 1, :] for k in range(kinds)], axis=1)
    down = jnp.concatenate([cols[:, k : k + 1] for k in range(kinds)], axis=0)
    owner_across = jnp.where(across >= 0, across >> 10, -1)
    owner_down = jnp.where(down >= 0, down >> 10, -2)
    first = lax.broadcasted_iota(I32, (total, total), 0)
    second = lax.broadcasted_iota(I32, (total, total), 1)
    same = (owner_down == owner_across) & (second < first)
    slot = jnp.sum(jnp.where(same, 1.0, 0.0), axis=1, keepdims=True).astype(I32)
    kind = jnp.where(lax.broadcasted_iota(I32, (total, 1), 0) < anchors, 0, 1024)
    code = (down & 1023) + kind + 1
    hit = (slot == lax.broadcasted_iota(I32, (total, 128), 1)) & (down >= 0)
    low = jnp.where(hit, code & 63, 0).astype(F32).astype(BF)
    high = jnp.where(hit, code >> 6, 0).astype(F32).astype(BF)
    devices = request_ref.shape[0]
    pick = jnp.where(owner_across == lax.broadcasted_iota(I32, (devices, total), 0), 1.0, 0.0).astype(BF)
    found = nn(pick, low) + 64.0 * nn(pick, high) - 1.0
    request_ref[...] = found[:, : request_ref.shape[1]].astype(I32)
    place = jnp.where(down >= 0, owner_down * 16 + slot, -1)
    for k in range(kinds):
        place_ref[:, k : k + 1] = place[k * anchors : (k + 1) * anchors]


def plan(rows, cols):
    return pl.pallas_call(
        plan_kernel,
        out_shape=(jax.ShapeDtypeStruct((128, 16), I32), jax.ShapeDtypeStruct(cols.shape, I32)),
        compiler_params=params(16),
        name="plan",
    )(rows, cols)


def serve_kernel(snap_ref, asked_ref, current_ref, following_ref, out_ref):
    asked = asked_ref[...]
    devices, lanes = asked.shape
    count = devices * MAIN
    wide = jnp.broadcast_to(asked[:, None, :], (devices, MAIN, lanes)).reshape(count, lanes)
    lane = lax.broadcasted_iota(I32, (count, lanes), 1)
    spot = lax.broadcasted_iota(I32, (count, lanes), 0) & (MAIN - 1)
    main = jnp.sum(jnp.where(lane == spot, wide, 0), axis=1, keepdims=True)
    spare = jnp.sum(jnp.where(lane == MAIN + (spot & (SPARE - 1)), wide, 0), axis=1, keepdims=True)
    nodes, width = current_ref.shape[1:]
    node = lax.broadcasted_iota(I32, (count, nodes), 1)

    def rows_of(code):
        now = jnp.where(node == code, 1.0, 0.0).astype(BF)
        later = jnp.where(node + nodes == code, 1.0, 0.0).astype(BF)
        return (nn(now, current_ref[0]) + nn(later, following_ref[0])).astype(BF)

    out_ref[:, :width] = rows_of(main)
    extra = rows_of(spare)
    half = width // 2
    upper = (lax.broadcasted_iota(I32, (count, half), 0) & (MAIN - 1)) < SPARE
    out_ref[:, width:] = jnp.where(upper, extra[:, :half].astype(F32), extra[:, half:].astype(F32)).astype(BF)


def serve(snapshot, asked, memory):
    devices, lanes = asked.shape
    _, nodes, width = memory.shape
    step = 32
    return pl.pallas_call(
        serve_kernel,
        grid_spec=pltpu.PrefetchScalarGridSpec(
            num_scalar_prefetch=1,
            grid=(devices // step,),
            in_specs=[
                pl.BlockSpec((step, lanes), lambda i, s: (i, 0)),
                pl.BlockSpec((1, nodes, width), lambda i, s: (s[0], 0, 0)),
                pl.BlockSpec((1, nodes, width), lambda i, s: (s[0] + 1, 0, 0)),
            ],
            out_specs=pl.BlockSpec((step * MAIN, width + width // 2), lambda i, s: (i, 0)),
        ),
        out_shape=jax.ShapeDtypeStruct((devices * MAIN, width + width // 2), BF),
        compiler_params=params(60),
        name="serve",
    )(snapshot, asked, memory, memory)


def unpack_kernel(scale, got_ref, place_ref, hidden_ref, count_ref, query_ref, positive_ref, logit_ref):
    anchors, kinds = place_ref.shape
    total, wide = got_ref.shape
    width = hidden_ref.shape[1]
    spot = lax.broadcasted_iota(I32, (anchors, total), 1)

    def masks(k):
        place = place_ref[:, k : k + 1]
        base, slot = (place >> 4) * MAIN, place & 15
        live = place >= 0
        main = jnp.where(live & (slot < MAIN), base + slot, -1)
        upper = jnp.where(live & (slot >= MAIN), base + slot - MAIN, -1)
        lower = jnp.where(live & (slot >= MAIN), base + slot - MAIN + SPARE, -1)
        return [jnp.where(spot == at, 1.0, 0.0) for at in (main, upper, lower)]

    first = masks(0)
    others = masks(1)
    for k in range(2, kinds):
        others = [a + b for a, b in zip(others, masks(k))]
    picks = [jnp.concatenate([a, b], axis=0).astype(BF) for a, b in zip(first, others)]
    rows = nn(picks[0], got_ref[:, :width])
    tail = got_ref[:, width:]
    rows = rows + jnp.concatenate([nn(picks[1], tail), nn(picks[2], tail)], axis=1)
    query = (hidden_ref[...].astype(F32) + rows[:anchors]).astype(BF)
    positive = (rows[anchors:] / count_ref[...].astype(F32)).astype(BF)
    query_ref[...] = query
    positive_ref[...] = positive
    logit_ref[...] = jnp.sum(query.astype(F32) * positive.astype(F32), axis=1, keepdims=True) * scale


def unpack(got, place, hidden, count, scale):
    anchors, width = hidden.shape
    return pl.pallas_call(
        functools.partial(unpack_kernel, scale),
        out_shape=(
            jax.ShapeDtypeStruct((anchors, width), BF),
            jax.ShapeDtypeStruct((anchors, width), BF),
            jax.ShapeDtypeStruct((anchors, 1), F32),
        ),
        compiler_params=params(16),
        name="unpack",
    )(got, place, hidden, count)


def score_kernel(unit, cand_ref, query_ref, logit_ref, top_ref, level_ref, part_ref):
    cands = cand_ref[...]
    logits = lax.dot_general(cands, query_ref[...], (((1,), (1,)), ((), ())), preferred_element_type=F32)
    logit_ref[...] = logits
    top = jnp.max(logits, axis=0, keepdims=True) * unit
    weights = jnp.exp2(logits * unit - top)
    top_ref[...] = top
    level_ref[...] = top + jnp.log2(jnp.sum(weights, axis=0, keepdims=True))
    part = lax.dot_general(weights.astype(BF), cands, (((0,), (0,)), ((), ())), preferred_element_type=F32)
    part_ref[...] = part


def score(cands, queries, unit):
    cand_count, width = cands.shape
    anchors = queries.shape[0]
    pairs = cand_count * anchors
    return pl.pallas_call(
        functools.partial(score_kernel, unit),
        out_shape=(
            jax.ShapeDtypeStruct((cand_count, anchors), F32),
            jax.ShapeDtypeStruct((1, anchors), F32),
            jax.ShapeDtypeStruct((1, anchors), F32),
            jax.ShapeDtypeStruct((anchors, width), F32),
        ),
        compiler_params=params(28),
        cost_estimate=cost(4 * pairs * width, 4 * pairs, pairs),
        name="score",
    )(cands, queries)


def cand_kernel(unit, *refs):
    logit_refs, (total_ref, query_ref, part_ref) = refs[:-3], refs[-3:]
    weights, start = [], 0
    for ref in logit_refs:
        stop = start + ref.shape[1]
        weights.append(jnp.exp2(ref[...] * unit - total_ref[:, start:stop]).astype(BF))
        start = stop
    part_ref[...] = nn(jnp.concatenate(weights, axis=1), query_ref[...]).astype(part_ref.dtype)


def cand_terms(logits, total, queries, first, count, kind, unit):
    anchors, width = queries.shape
    start = first // TILE
    pairs = count * anchors
    return pl.pallas_call(
        functools.partial(cand_kernel, unit),
        grid=(count // TILE,),
        in_specs=[pl.BlockSpec((TILE, part.shape[1]), lambda i: (i + start, 0)) for part in logits]
        + [
            pl.BlockSpec((1, anchors), lambda i: (0, 0)),
            pl.BlockSpec((anchors, width), lambda i: (0, 0)),
        ],
        out_specs=pl.BlockSpec((TILE, width), lambda i: (i, 0)),
        out_shape=jax.ShapeDtypeStruct((count, width), kind),
        compiler_params=params(28),
        cost_estimate=cost(2 * pairs * width, 4 * pairs, pairs),
        name="cand_terms",
    )(*logits, total, queries)


def merge(levels):
    top = functools.reduce(jnp.maximum, levels)
    return top + jnp.log2(sum(jnp.exp2(level - top) for level in levels))


def table_kernel(*refs):
    level_refs, (logit_ref, table_ref) = refs[:-2], refs[-2:]
    half = table_ref.shape[1] // 2
    rows = []
    for x in range(SIDE):
        for z in range(SIDE):
            a_part = level_refs[x][:, z * half : (z + 1) * half]
            b_part = level_refs[z][:, (SIDE + x) * half : (SIDE + x + 1) * half]
            rows.append(jnp.concatenate([a_part, b_part], axis=1))
    rows[0] = merge([rows[0], logit_ref[...] * math.log2(math.e)])
    table_ref[...] = jnp.concatenate(rows, axis=0)


def table(levels, pos_logit, anchors):
    return pl.pallas_call(
        table_kernel,
        out_shape=jax.ShapeDtypeStruct((SIDE * SIDE, anchors), F32),
        compiler_params=params(8),
        name="level_table",
    )(*levels, pos_logit)


def rolled(value, along_x, by):
    if along_x:
        cut = (SIDE - by) * SIDE
        return jnp.concatenate([value[cut:], value[:cut]], axis=0)
    rows = []
    for x in range(SIDE):
        cut = x * SIDE + SIDE - by
        rows += [value[cut : (x + 1) * SIDE], value[x * SIDE : cut]]
    return jnp.concatenate(rows, axis=0)


def merge_kernel(along_x, own_ref, *refs):
    came_refs, out_ref = refs[:-1], refs[-1]
    levels = [own_ref[...]]
    for by, ref in zip((1, 2, 3), came_refs):
        levels.append(rolled(ref[...], along_x, by))
    out_ref[...] = merge(levels)


def merged(own, came, along_x):
    return pl.pallas_call(
        functools.partial(merge_kernel, along_x),
        out_shape=jax.ShapeDtypeStruct(own.shape, F32),
        compiler_params=params(8),
        name="level_merge",
    )(own, *came)


def spread_kernel(own_ref, *refs):
    came_refs, top_refs, (total_ref, factor_ref, log_ref) = refs[:3], refs[3:7], refs[7:]
    levels = [own_ref[...]]
    for by, ref in zip((1, 2, 3), came_refs):
        levels.append(rolled(ref[...], True, by))
    table = merge(levels)
    half = table.shape[1] // 2
    for j in range(SIDE):
        a_parts = [table[j * SIDE + i : j * SIDE + i + 1, :half] for i in range(SIDE)]
        b_parts = [table[i * SIDE + j : i * SIDE + j + 1, half:] for i in range(SIDE)]
        row = jnp.concatenate(a_parts + b_parts, axis=1)
        size = row.shape[1]
        total_ref[:, j * size : (j + 1) * size] = row
        factor_ref[:, j * size : (j + 1) * size] = jnp.exp2(top_refs[j][...] - row)
    log_ref[...] = table[0:1] * math.log(2.0)


def spread(own, came, tops):
    groups, anchors = own.shape
    return pl.pallas_call(
        spread_kernel,
        out_shape=(
            jax.ShapeDtypeStruct((1, groups * anchors), F32),
            jax.ShapeDtypeStruct((1, groups * anchors), F32),
            jax.ShapeDtypeStruct((1, anchors), F32),
        ),
        compiler_params=params(8),
        name="level_spread",
    )(own, *came, *tops)


def body(anchor_hidden, candidates, memory, anchor_ids, pos_ids, pos_count, snapshot):
    anchors, width = anchor_hidden.shape
    scale = 1.0 / math.sqrt(width)
    unit = scale * math.log2(math.e)
    half = anchors // 2
    steps = (1, 2, 3)

    along_y = [shift_y(candidates, d) for d in steps]

    ids = jnp.concatenate([anchor_ids[:, None], pos_ids], axis=1)
    requests, place = plan(ids.T, ids)
    asked = lax.all_to_all(requests, ("row", "col"), split_axis=0, concat_axis=0, tiled=True)
    asked, *along_y = lax.optimization_barrier((asked, *along_y))
    along_y = jnp.concatenate([candidates] + along_y, axis=0)
    cands = jnp.concatenate([along_y, swap_core(along_y)], axis=0)
    served = serve(snapshot, asked, memory)
    devices = asked.shape[0]
    served = served.reshape(devices, MAIN, served.shape[1])
    got = lax.all_to_all(served, ("row", "col"), split_axis=0, concat_axis=0, tiled=True)
    got = got.reshape(devices * MAIN, got.shape[2])
    query, positive, pos_logit = unpack(got, place, anchor_hidden, pos_count[:, None], scale)
    pos_logit = pos_logit.reshape(anchors)

    first, second = query[:half], query[half:]
    first = jnp.concatenate([first] + [shift_z(first, d) for d in steps], axis=0)
    second = jnp.concatenate([second] + [shift_x(second, d) for d in steps], axis=0)
    first, second = lax.optimization_barrier((first, second))
    groups = [jnp.concatenate([first, second], axis=0)]
    for d in (1, 3, 2):
        groups.append(jnp.concatenate([shift_x(first, d), shift_z(second, d)], axis=0))
    groups = [groups[0], groups[1], groups[3], groups[2]]
    scored = [score(cands, group, unit) for group in groups]
    logits = [one[0] for one in scored]
    tops = [one[1] for one in scored]
    levels = [one[2] for one in scored]
    parts = [one[3] for one in scored]

    known = table(levels, pos_logit.reshape(1, anchors), anchors)
    known = merged(known, [shift_z(known, d) for d in steps], False)
    total, factor, log_total = spread(known, [shift_x(known, d) for d in steps], tops)
    log_total = log_total.reshape(anchors)
    factors = factor.reshape(SIDE, -1)

    queries = jnp.concatenate(groups, axis=0)
    size = SIDE * half
    scaled = [part * factors[j][:, None] for j, part in enumerate(parts)]
    a_came = [shift_x(scaled[d][:size].astype(BF), -d) for d in steps]
    b_came = [shift_z(scaled[d][size:].astype(BF), -d) for d in steps]

    total, a_came[0] = lax.optimization_barrier((total, a_came[0]))
    count = cands.shape[0] // 2
    away = cand_terms(logits, total, queries, count, count, BF, unit)
    total, away = lax.optimization_barrier((total, away))
    came = swap_core(away).astype(F32)
    home = cand_terms(logits, total, queries, 0, count, F32, unit)
    shard = candidates.shape[0]
    held = [home[d * shard : (d + 1) * shard] + came[d * shard : (d + 1) * shard] for d in range(SIDE)]
    cand_grad = held[0]
    for d in steps:
        cand_grad = cand_grad + shift_y(held[d].astype(BF), -d).astype(F32)

    a_sum, b_sum = scaled[0][:size], scaled[0][size:]
    for one, other in zip(a_came, b_came):
        a_sum = a_sum + one.astype(F32)
        b_sum = b_sum + other.astype(F32)
    a_all, b_all = a_sum[:half], b_sum[:half]
    for d in steps:
        a_all = a_all + shift_z(a_sum[d * half : (d + 1) * half].astype(BF), -d).astype(F32)
        b_all = b_all + shift_x(b_sum[d * half : (d + 1) * half].astype(BF), -d).astype(F32)
    weighted = jnp.concatenate([a_all, b_all], axis=0)
    anchor_grad = weighted + (jnp.exp(pos_logit - log_total) - 1.0)[:, None] * positive.astype(F32)
    loss = log_total - pos_logit

    return (loss, anchor_grad, cand_grad)


def solution(mesh):
    in_specs = (
        P(("row", "col"), None),
        P(("col", "row"), None),
        P(None, ("row", "col"), None),
        P(("row", "col")),
        P(("row", "col"), None),
        P(("row", "col")),
        P(),
    )
    out_specs = (P(("row", "col")), P(("row", "col"), None), P(("col", "row"), None))
    return jax.shard_map(body, mesh=mesh, in_specs=in_specs, out_specs=out_specs, check_vma=False)
```

```python
import functools
import math

import jax
import jax.numpy as jnp
from jax import lax
from jax.experimental import pallas as pl
from jax.experimental.pallas import tpu as pltpu
from jax.sharding import PartitionSpec as P

BF = jnp.bfloat16
F32 = jnp.float32
I32 = jnp.int32
SIDE = 4
MIB = 1024 * 1024
MAIN = 8
SPARE = 4
TILE = 512
CHUNK = 256
LABEL = 16


def params(mib):
    return pltpu.CompilerParams(vmem_limit_bytes=mib * MIB)


def cost(flops, moved, exps=0):
    return pl.CostEstimate(flops=1, bytes_accessed=1, transcendentals=0)


def nn(a, b):
    return jnp.dot(a, b, preferred_element_type=F32)


def shift_x(value, by):
    pairs = [(x * SIDE + z, (x + by) % SIDE * SIDE + z) for x in range(SIDE) for z in range(SIDE)]
    return lax.ppermute(value, "row", pairs)


def shift_z(value, by):
    pairs = [(x * SIDE + z, x * SIDE + (z + by) % SIDE) for x in range(SIDE) for z in range(SIDE)]
    return lax.ppermute(value, "row", pairs)


def shift_y(value, by):
    pairs = [(y * 2 + k, (y + by) % SIDE * 2 + k) for y in range(SIDE) for k in range(2)]
    return lax.ppermute(value, "col", pairs)


def swap_core(value):
    return lax.ppermute(value, "col", [(i, i ^ 1) for i in range(2 * SIDE)])


def plan_kernel(rows_ref, cols_ref, request_ref, place_ref):
    rows, cols = rows_ref[...], cols_ref[...]
    kinds, anchors = rows.shape
    total = kinds * anchors
    across = jnp.concatenate([rows[k : k + 1, :] for k in range(kinds)], axis=1)
    down = jnp.concatenate([cols[:, k : k + 1] for k in range(kinds)], axis=0)
    owner_across = jnp.where(across >= 0, across >> 10, -1)
    owner_down = jnp.where(down >= 0, down >> 10, -2)
    first = lax.broadcasted_iota(I32, (total, total), 0)
    second = lax.broadcasted_iota(I32, (total, total), 1)
    same = (owner_down == owner_across) & (second < first)
    slot = jnp.sum(jnp.where(same, 1.0, 0.0), axis=1, keepdims=True).astype(I32)
    kind = jnp.where(lax.broadcasted_iota(I32, (total, 1), 0) < anchors, 0, 1024)
    code = (down & 1023) + kind + 1
    hit = (slot == lax.broadcasted_iota(I32, (total, 128), 1)) & (down >= 0)
    low = jnp.where(hit, code & 63, 0).astype(F32).astype(BF)
    high = jnp.where(hit, code >> 6, 0).astype(F32).astype(BF)
    devices = request_ref.shape[0]
    pick = jnp.where(owner_across == lax.broadcasted_iota(I32, (devices, total), 0), 1.0, 0.0).astype(BF)
    found = nn(pick, low) + 64.0 * nn(pick, high) - 1.0
    request_ref[...] = found[:, : request_ref.shape[1]].astype(I32)
    place = jnp.where(down >= 0, owner_down * 16 + slot, -1)
    for k in range(kinds):
        place_ref[:, k : k + 1] = place[k * anchors : (k + 1) * anchors]


def plan(rows, cols):
    return pl.pallas_call(
        plan_kernel,
        out_shape=(jax.ShapeDtypeStruct((128, 16), I32), jax.ShapeDtypeStruct(cols.shape, I32)),
        compiler_params=params(16),
        name="plan",
    )(rows, cols)


def serve_kernel(snap_ref, asked_ref, current_ref, following_ref, out_ref):
    asked = asked_ref[...]
    devices, lanes = asked.shape
    count = devices * MAIN
    wide = jnp.broadcast_to(asked[:, None, :], (devices, MAIN, lanes)).reshape(count, lanes)
    lane = lax.broadcasted_iota(I32, (count, lanes), 1)
    spot = lax.broadcasted_iota(I32, (count, lanes), 0) & (MAIN - 1)
    main = jnp.sum(jnp.where(lane == spot, wide, 0), axis=1, keepdims=True)
    spare = jnp.sum(jnp.where(lane == MAIN + (spot & (SPARE - 1)), wide, 0), axis=1, keepdims=True)
    nodes, width = current_ref.shape[1:]
    node = lax.broadcasted_iota(I32, (count, nodes), 1)

    def rows_of(code):
        now = jnp.where(node == code, 1.0, 0.0).astype(BF)
        later = jnp.where(node + nodes == code, 1.0, 0.0).astype(BF)
        return (nn(now, current_ref[0]) + nn(later, following_ref[0])).astype(BF)

    out_ref[:, :width] = rows_of(main)
    extra = rows_of(spare)
    half = width // 2
    upper = (lax.broadcasted_iota(I32, (count, half), 0) & (MAIN - 1)) < SPARE
    out_ref[:, width:] = jnp.where(upper, extra[:, :half].astype(F32), extra[:, half:].astype(F32)).astype(BF)


def serve(snapshot, asked, memory):
    devices, lanes = asked.shape
    _, nodes, width = memory.shape
    step = 32
    return pl.pallas_call(
        serve_kernel,
        grid_spec=pltpu.PrefetchScalarGridSpec(
            num_scalar_prefetch=1,
            grid=(devices // step,),
            in_specs=[
                pl.BlockSpec((step, lanes), lambda i, s: (i, 0)),
                pl.BlockSpec((1, nodes, width), lambda i, s: (s[0], 0, 0)),
                pl.BlockSpec((1, nodes, width), lambda i, s: (s[0] + 1, 0, 0)),
            ],
            out_specs=pl.BlockSpec((step * MAIN, width + width // 2), lambda i, s: (i, 0)),
        ),
        out_shape=jax.ShapeDtypeStruct((devices * MAIN, width + width // 2), BF),
        compiler_params=params(60),
        name="serve",
    )(snapshot, asked, memory, memory)


def unpack_kernel(scale, got_ref, place_ref, hidden_ref, count_ref, query_ref, positive_ref, logit_ref):
    anchors, kinds = place_ref.shape
    total, wide = got_ref.shape
    width = hidden_ref.shape[1]
    spot = lax.broadcasted_iota(I32, (anchors, total), 1)

    def masks(k):
        place = place_ref[:, k : k + 1]
        base, slot = (place >> 4) * MAIN, place & 15
        live = place >= 0
        main = jnp.where(live & (slot < MAIN), base + slot, -1)
        upper = jnp.where(live & (slot >= MAIN), base + slot - MAIN, -1)
        lower = jnp.where(live & (slot >= MAIN), base + slot - MAIN + SPARE, -1)
        return [jnp.where(spot == at, 1.0, 0.0) for at in (main, upper, lower)]

    first = masks(0)
    others = masks(1)
    for k in range(2, kinds):
        others = [a + b for a, b in zip(others, masks(k))]
    picks = [jnp.concatenate([a, b], axis=0).astype(BF) for a, b in zip(first, others)]
    rows = nn(picks[0], got_ref[:, :width])
    tail = got_ref[:, width:]
    rows = rows + jnp.concatenate([nn(picks[1], tail), nn(picks[2], tail)], axis=1)
    query = (hidden_ref[...].astype(F32) + rows[:anchors]).astype(BF)
    positive = (rows[anchors:] / count_ref[...].astype(F32)).astype(BF)
    query_ref[...] = query
    positive_ref[...] = positive
    logit_ref[...] = jnp.sum(query.astype(F32) * positive.astype(F32), axis=1, keepdims=True) * scale


def unpack(got, place, hidden, count, scale):
    anchors, width = hidden.shape
    return pl.pallas_call(
        functools.partial(unpack_kernel, scale),
        out_shape=(
            jax.ShapeDtypeStruct((anchors, width), BF),
            jax.ShapeDtypeStruct((anchors, width), BF),
            jax.ShapeDtypeStruct((anchors, 1), F32),
        ),
        compiler_params=params(16),
        name="unpack",
    )(got, place, hidden, count)


def score_kernel(unit, near_ref, far_ref, *refs):
    pieces = (len(refs) - 4) // 2
    piece_refs, (logit_ref, level_ref, query_ref) = refs[:pieces], refs[pieces : pieces + 3]
    sent_refs, sems = refs[pieces + 3 : -1], refs[-1]
    step = pl.program_id(0)
    size = piece_refs[0].shape[0]
    copies = [
        pltpu.make_async_copy(ref, query_ref.at[pl.ds(k * size, size), :], sems.at[k])
        for k, ref in enumerate(piece_refs)
    ]

    @pl.when(step == 0)
    def _():
        for copy in copies:
            copy.start()

    for g in range(len(copies) // 2):

        @pl.when(step == g)
        def _():
            copies[2 * g].wait()
            copies[2 * g + 1].wait()

    queries = query_ref[pl.ds(pl.multiple_of(step * 2 * size, 2 * size), 2 * size), :]
    count = near_ref.shape[0]
    chunks = [(ref, row) for ref in (near_ref, far_ref) for row in range(0, count, CHUNK)]
    top = None
    for j, (ref, row) in enumerate(chunks):
        logits = lax.dot_general(
            ref[row : row + CHUNK, :], queries, (((1,), (1,)), ((), ())), preferred_element_type=F32
        )
        logit_ref[j * CHUNK : (j + 1) * CHUNK, :] = logits
        peak = jnp.max(logits, axis=0, keepdims=True)
        top = peak if top is None else jnp.maximum(top, peak)
    top = (top * unit).astype(BF).astype(F32)
    total, weights = 0.0, []
    for j in range(len(chunks)):
        one = jnp.exp2(logit_ref[j * CHUNK : (j + 1) * CHUNK, :] * unit - top)
        total = total + jnp.sum(one, axis=0, keepdims=True)
        weights.append(one.astype(BF))
    half = len(weights) // 2
    part = 0.0
    for ref, some in ((near_ref, weights[:half]), (far_ref, weights[half:])):
        turned = (((0,), (0,)), ((), ()))
        part = part + lax.dot_general(jnp.concatenate(some, axis=0), ref[...], turned, preferred_element_type=F32)
    level_ref[...] = top + jnp.log2(total)
    part, width = part.astype(BF), part.shape[1]
    blank = jnp.zeros((LABEL, width - size), F32)
    for g in range(pieces // 2):

        @pl.when(step == g)
        def _():
            for h in range(2):
                cut = slice(h * size, (h + 1) * size)
                label = jnp.broadcast_to(top[:, cut], (LABEL, size))
                sent_refs[2 * g + h][:size, :] = part[cut]
                sent_refs[2 * g + h][size:, :] = jnp.concatenate([label, blank], axis=1).astype(BF)


def score(near, far, pieces, unit):
    cand_count, width = 2 * near.shape[0], near.shape[1]
    groups, each = len(pieces) // 2, 2 * pieces[0].shape[0]
    anchors = groups * each
    pairs = cand_count * anchors
    return pl.pallas_call(
        functools.partial(score_kernel, unit),
        grid=(groups,),
        in_specs=[pl.BlockSpec(near.shape, lambda i: (0, 0))] * 2
        + [pl.BlockSpec(memory_space=pl.ANY) for _ in pieces],
        out_specs=(
            pl.BlockSpec((cand_count, each), lambda i: (0, i)),
            pl.BlockSpec((1, each), lambda i: (0, i)),
            pl.BlockSpec((anchors, width), lambda i: (0, 0)),
        )
        + (pl.BlockSpec((each // 2 + LABEL, width), lambda i: (0, 0)),) * len(pieces),
        out_shape=(
            jax.ShapeDtypeStruct((cand_count, anchors), F32),
            jax.ShapeDtypeStruct((1, anchors), F32),
            jax.ShapeDtypeStruct((anchors, width), BF),
        )
        + (jax.ShapeDtypeStruct((each // 2 + LABEL, width), BF),) * len(pieces),
        scratch_shapes=[pltpu.SemaphoreType.DMA((len(pieces),))],
        compiler_params=params(56),
        cost_estimate=cost(4 * pairs * width, 4 * pairs, pairs),
        name="score",
    )(near, far, *pieces)


def cand_kernel(unit, own_ref, rest_ref, total_ref, own_query_ref, rest_query_ref, part_ref):
    split = own_ref.shape[1]
    part = 0.0
    for ref, query_ref, cut in (
        (own_ref, own_query_ref, slice(0, split)),
        (rest_ref, rest_query_ref, slice(split, None)),
    ):
        weights = jnp.exp2(ref[...] * unit - total_ref[:, cut]).astype(BF)
        part = part + nn(weights, query_ref[...])
    part_ref[...] = part.astype(part_ref.dtype)


def cand_terms(logits, total, queries, first, count, kind, unit):
    width = queries[0].shape[1]
    anchors = total.shape[1]
    start = first // TILE
    pairs = count * anchors
    return pl.pallas_call(
        functools.partial(cand_kernel, unit),
        grid=(count // TILE,),
        in_specs=[pl.BlockSpec((TILE, part.shape[1]), lambda i: (i + start, 0)) for part in logits]
        + [pl.BlockSpec((1, anchors), lambda i: (0, 0))]
        + [pl.BlockSpec(part.shape, lambda i: (0, 0)) for part in queries],
        out_specs=pl.BlockSpec((TILE, width), lambda i: (i, 0)),
        out_shape=jax.ShapeDtypeStruct((count, width), kind),
        compiler_params=params(60),
        cost_estimate=cost(2 * pairs * width, 4 * pairs, pairs),
        name="cand_terms",
    )(*logits, total, *queries)


def merge(levels):
    top = functools.reduce(jnp.maximum, levels)
    return top + jnp.log2(sum(jnp.exp2(level - top) for level in levels))


def table_kernel(*refs):
    level_refs, (logit_ref, table_ref) = refs[:-2], refs[-2:]
    levels = jnp.concatenate([ref[...] for ref in level_refs], axis=1)
    half = table_ref.shape[1] // 2
    size = 2 * SIDE * half
    rows = []
    for x in range(SIDE):
        for z in range(SIDE):
            a_part = levels[:, x * size + z * half : x * size + (z + 1) * half]
            b_part = levels[:, z * size + (SIDE + x) * half : z * size + (SIDE + x + 1) * half]
            rows.append(jnp.concatenate([a_part, b_part], axis=1))
    rows[0] = merge([rows[0], logit_ref[...] * math.log2(math.e)])
    table_ref[...] = jnp.concatenate(rows, axis=0)


def table(levels, pos_logit, anchors):
    return pl.pallas_call(
        table_kernel,
        out_shape=jax.ShapeDtypeStruct((SIDE * SIDE, anchors), F32),
        compiler_params=params(8),
        name="level_table",
    )(*levels, pos_logit)


def rolled(value, along_x, by):
    if along_x:
        cut = (SIDE - by) * SIDE
        return jnp.concatenate([value[cut:], value[:cut]], axis=0)
    rows = []
    for x in range(SIDE):
        cut = x * SIDE + SIDE - by
        rows += [value[cut : (x + 1) * SIDE], value[x * SIDE : cut]]
    return jnp.concatenate(rows, axis=0)


def merge_kernel(along_x, own_ref, *refs):
    came_refs, out_ref = refs[:-1], refs[-1]
    levels = [own_ref[...]]
    for by, ref in zip((1, 2, 3), came_refs):
        levels.append(rolled(ref[...], along_x, by))
    out_ref[...] = merge(levels)


def merged(own, came, along_x):
    return pl.pallas_call(
        functools.partial(merge_kernel, along_x),
        out_shape=jax.ShapeDtypeStruct(own.shape, F32),
        compiler_params=params(8),
        name="level_merge",
    )(own, *came)


def spread_kernel(own_ref, *refs):
    came_refs, (total_ref, log_ref) = refs[:3], refs[3:]
    levels = [own_ref[...]]
    for by, ref in zip((1, 2, 3), came_refs):
        levels.append(rolled(ref[...], True, by))
    table = merge(levels)
    half = table.shape[1] // 2
    for j in range(SIDE):
        a_parts = [table[j * SIDE + i : j * SIDE + i + 1, :half] for i in range(SIDE)]
        b_parts = [table[i * SIDE + j : i * SIDE + j + 1, half:] for i in range(SIDE)]
        row = jnp.concatenate(a_parts + b_parts, axis=1)
        size = row.shape[1]
        total_ref[:, j * size : (j + 1) * size] = row
    log_ref[...] = table[0:1] * math.log(2.0)


def spread(own, came):
    groups, anchors = own.shape
    return pl.pallas_call(
        spread_kernel,
        out_shape=(
            jax.ShapeDtypeStruct((1, groups * anchors), F32),
            jax.ShapeDtypeStruct((1, anchors), F32),
        ),
        compiler_params=params(8),
        name="level_spread",
    )(own, *came)


def combine_kernel(total_ref, *refs):
    piece_refs, out_refs = refs[: 2 * SIDE], refs[2 * SIDE :]
    rows = piece_refs[0].shape[0] - LABEL
    half = rows // SIDE
    for h in range(2):
        total = total_ref[:, h * rows : (h + 1) * rows]
        joined = 0.0
        for ref in piece_refs[h * SIDE : (h + 1) * SIDE]:
            level = ref[rows:, :rows].astype(F32)[:8]
            factor = jnp.exp2(level - total).T[:, :1]
            joined = joined + ref[:rows, :].astype(F32) * factor
        for d in range(SIDE):
            out_ref = out_refs[h * SIDE + d]
            out_ref[...] = joined[d * half : (d + 1) * half].astype(out_ref.dtype)


def combine(total, pieces):
    rows, width = pieces[0].shape
    half = (rows - LABEL) // SIDE
    one = tuple(jax.ShapeDtypeStruct((half, width), F32 if d == 0 else BF) for d in range(SIDE))
    return pl.pallas_call(
        combine_kernel,
        out_shape=one + one,
        compiler_params=params(40),
        name="combine",
    )(total, *pieces)


def body(anchor_hidden, candidates, memory, anchor_ids, pos_ids, pos_count, snapshot):
    anchors, width = anchor_hidden.shape
    scale = 1.0 / math.sqrt(width)
    unit = scale * math.log2(math.e)
    half = anchors // 2
    steps = (1, 2, 3)

    along_y = [shift_y(candidates, d) for d in steps]

    ids = jnp.concatenate([anchor_ids[:, None], pos_ids], axis=1)
    requests, place = plan(ids.T, ids)
    asked = lax.all_to_all(requests, ("row", "col"), split_axis=0, concat_axis=0, tiled=True)
    asked, *along_y = lax.optimization_barrier((asked, *along_y))
    along_y = jnp.concatenate([candidates] + along_y, axis=0)
    near, far = along_y, swap_core(along_y)
    served = serve(snapshot, asked, memory)
    devices = asked.shape[0]
    served = served.reshape(devices, MAIN, served.shape[1])
    got = lax.all_to_all(served, ("row", "col"), split_axis=0, concat_axis=0, tiled=True)
    got = got.reshape(devices * MAIN, got.shape[2])
    query, positive, pos_logit = unpack(got, place, anchor_hidden, pos_count[:, None], scale)
    pos_logit = pos_logit.reshape(anchors)

    first, second = query[:half], query[half:]
    first = jnp.concatenate([first] + [shift_z(first, d) for d in steps], axis=0)
    second = jnp.concatenate([second] + [shift_x(second, d) for d in steps], axis=0)
    first, second = lax.optimization_barrier((first, second))
    pieces = []
    for d in steps:
        pieces += [shift_x(first, d), shift_z(second, d)]
    scored = [score(near, far, [first, second], unit)]
    _, *pieces = lax.optimization_barrier((scored[0][1], *pieces))
    scored.append(score(near, far, pieces, unit))
    logits, levels, queries = zip(*(one[:3] for one in scored))
    own_a, own_b = scored[0][3:]
    sent = [None] + [list(scored[1][2 * d + 1 : 2 * d + 3]) for d in steps]
    a_came = {d: shift_x(sent[d][0], -d) for d in (1, 3)}
    b_came = {d: shift_z(sent[d][1], -d) for d in (1, 3)}

    known = table(levels, pos_logit.reshape(1, anchors), anchors)
    known = merged(known, [shift_z(known, d) for d in steps], False)
    total, log_total = spread(known, [shift_x(known, d) for d in steps])
    log_total = log_total.reshape(anchors)

    count = near.shape[0]
    away = cand_terms(logits, total, queries, count, count, BF, unit)
    total, away = lax.optimization_barrier((total, away))
    came = swap_core(away).astype(F32)
    home = cand_terms(logits, total, queries, 0, count, F32, unit)
    home, *sent[2] = lax.optimization_barrier((home, *sent[2]))
    a_came[2], b_came[2] = shift_x(sent[2][0], -2), shift_z(sent[2][1], -2)
    shard = candidates.shape[0]
    held = [home[d * shard : (d + 1) * shard] + came[d * shard : (d + 1) * shard] for d in range(SIDE)]
    moved = [shift_y(held[d].astype(BF), -d) for d in steps]
    total, moved[0] = lax.optimization_barrier((total, moved[0]))
    cand_grad = held[0]
    for one in moved:
        cand_grad = cand_grad + one.astype(F32)

    summed = combine(total, [own_a] + [a_came[d] for d in steps] + [own_b] + [b_came[d] for d in steps])
    a_all, b_all = summed[0], summed[SIDE]
    for d in steps:
        a_all = a_all + shift_z(summed[d], -d).astype(F32)
        b_all = b_all + shift_x(summed[SIDE + d], -d).astype(F32)
    weighted = jnp.concatenate([a_all, b_all], axis=0)
    anchor_grad = weighted + (jnp.exp(pos_logit - log_total) - 1.0)[:, None] * positive.astype(F32)
    loss = log_total - pos_logit

    return (loss, anchor_grad, cand_grad)


def solution(mesh):
    in_specs = (
        P(("row", "col"), None),
        P(("col", "row"), None),
        P(None, ("row", "col"), None),
        P(("row", "col")),
        P(("row", "col"), None),
        P(("row", "col")),
        P(),
    )
    out_specs = (P(("row", "col")), P(("row", "col"), None), P(("col", "row"), None))
    return jax.shard_map(body, mesh=mesh, in_specs=in_specs, out_specs=out_specs, check_vma=False)
```

```python
import functools
import math

import jax
import jax.numpy as jnp
from jax import lax
from jax.experimental import pallas as pl
from jax.experimental.pallas import tpu as pltpu
from jax.sharding import PartitionSpec as P

BF = jnp.bfloat16
F32 = jnp.float32
I32 = jnp.int32
SIDE = 4
MIB = 1024 * 1024
MAIN = 8
SPARE = 4
TILE = 512
CHUNK = 256
LABEL = 16
ORDER = (0, 1, 3, 2)


def params(mib):
    return pltpu.CompilerParams(vmem_limit_bytes=mib * MIB)


def cost(flops, moved, exps=0):
    return pl.CostEstimate(flops=1, bytes_accessed=1, transcendentals=0)


def nn(a, b):
    return jnp.dot(a, b, preferred_element_type=F32)


def shift_x(value, by):
    pairs = [(x * SIDE + z, (x + by) % SIDE * SIDE + z) for x in range(SIDE) for z in range(SIDE)]
    return lax.ppermute(value, "row", pairs)


def shift_z(value, by):
    pairs = [(x * SIDE + z, x * SIDE + (z + by) % SIDE) for x in range(SIDE) for z in range(SIDE)]
    return lax.ppermute(value, "row", pairs)


def shift_y(value, by):
    pairs = [(y * 2 + k, (y + by) % SIDE * 2 + k) for y in range(SIDE) for k in range(2)]
    return lax.ppermute(value, "col", pairs)


def swap_core(value):
    return lax.ppermute(value, "col", [(i, i ^ 1) for i in range(2 * SIDE)])


def plan_kernel(rows_ref, cols_ref, request_ref, place_ref):
    rows, cols = rows_ref[...], cols_ref[...]
    kinds, anchors = rows.shape
    total = kinds * anchors
    across = jnp.concatenate([rows[k : k + 1, :] for k in range(kinds)], axis=1)
    down = jnp.concatenate([cols[:, k : k + 1] for k in range(kinds)], axis=0)
    owner_across = jnp.where(across >= 0, across >> 10, -1)
    owner_down = jnp.where(down >= 0, down >> 10, -2)
    first = lax.broadcasted_iota(I32, (total, total), 0)
    second = lax.broadcasted_iota(I32, (total, total), 1)
    same = (owner_down == owner_across) & (second < first)
    slot = jnp.sum(jnp.where(same, 1.0, 0.0), axis=1, keepdims=True).astype(I32)
    kind = jnp.where(lax.broadcasted_iota(I32, (total, 1), 0) < anchors, 0, 1024)
    code = (down & 1023) + kind + 1
    hit = (slot == lax.broadcasted_iota(I32, (total, 128), 1)) & (down >= 0)
    low = jnp.where(hit, code & 63, 0).astype(F32).astype(BF)
    high = jnp.where(hit, code >> 6, 0).astype(F32).astype(BF)
    devices = request_ref.shape[0]
    pick = jnp.where(owner_across == lax.broadcasted_iota(I32, (devices, total), 0), 1.0, 0.0).astype(BF)
    found = nn(pick, low) + 64.0 * nn(pick, high) - 1.0
    request_ref[...] = found[:, : request_ref.shape[1]].astype(I32)
    place = jnp.where(down >= 0, owner_down * 16 + slot, -1)
    for k in range(kinds):
        place_ref[:, k : k + 1] = place[k * anchors : (k + 1) * anchors]


def plan(rows, cols):
    return pl.pallas_call(
        plan_kernel,
        out_shape=(jax.ShapeDtypeStruct((128, 16), I32), jax.ShapeDtypeStruct(cols.shape, I32)),
        compiler_params=params(16),
        name="plan",
    )(rows, cols)


def serve_kernel(snap_ref, asked_ref, current_ref, following_ref, out_ref):
    asked = asked_ref[...]
    devices, lanes = asked.shape
    nodes, width = current_ref.shape[1:]

    def rows_of(first, slots):
        count = devices * slots
        wide = jnp.broadcast_to(asked[:, None, :], (devices, slots, lanes)).reshape(count, lanes)
        lane = lax.broadcasted_iota(I32, (count, lanes), 1)
        spot = lax.broadcasted_iota(I32, (count, lanes), 0) & (slots - 1)
        code = jnp.sum(jnp.where(lane == first + spot, wide, 0), axis=1, keepdims=True)
        node = lax.broadcasted_iota(I32, (count, nodes), 1)
        now = jnp.where(node == code, 1.0, 0.0).astype(BF)
        later = jnp.where(node + nodes == code, 1.0, 0.0).astype(BF)
        return (nn(now, current_ref[0]) + nn(later, following_ref[0])).astype(BF)

    out_ref[:, :width] = rows_of(0, MAIN)
    extra = rows_of(MAIN, SPARE)
    half = width // 2
    row = lax.broadcasted_iota(I32, (devices * MAIN, devices * SPARE), 0)
    column = lax.broadcasted_iota(I32, (devices * MAIN, devices * SPARE), 1)
    spot = row & (MAIN - 1)
    match = (row >> 3) * SPARE + (spot & (SPARE - 1)) == column
    upper = jnp.where(match & (spot < SPARE), 1.0, 0.0).astype(BF)
    lower = jnp.where(match & (spot >= SPARE), 1.0, 0.0).astype(BF)
    out_ref[:, width:] = (nn(upper, extra[:, :half]) + nn(lower, extra[:, half:])).astype(BF)


def serve(snapshot, asked, memory):
    devices, lanes = asked.shape
    _, nodes, width = memory.shape
    step = 64
    return pl.pallas_call(
        serve_kernel,
        grid_spec=pltpu.PrefetchScalarGridSpec(
            num_scalar_prefetch=1,
            grid=(devices // step,),
            in_specs=[
                pl.BlockSpec((step, lanes), lambda i, s: (i, 0)),
                pl.BlockSpec((1, nodes, width), lambda i, s: (s[0], 0, 0)),
                pl.BlockSpec((1, nodes, width), lambda i, s: (s[0] + 1, 0, 0)),
            ],
            out_specs=pl.BlockSpec((step * MAIN, width + width // 2), lambda i, s: (i, 0)),
        ),
        out_shape=jax.ShapeDtypeStruct((devices * MAIN, width + width // 2), BF),
        compiler_params=params(60),
        name="serve",
    )(snapshot, asked, memory, memory)


def unpack_kernel(scale, got_ref, place_ref, hidden_ref, count_ref, query_ref, positive_ref, logit_ref):
    anchors, kinds = place_ref.shape
    total, wide = got_ref.shape
    width = hidden_ref.shape[1]
    spot = lax.broadcasted_iota(I32, (anchors, total), 1)

    def masks(k):
        place = place_ref[:, k : k + 1]
        base, slot = (place >> 4) * MAIN, place & 15
        live = place >= 0
        main = jnp.where(live & (slot < MAIN), base + slot, -1)
        upper = jnp.where(live & (slot >= MAIN), base + slot - MAIN, -1)
        lower = jnp.where(live & (slot >= MAIN), base + slot - MAIN + SPARE, -1)
        return [jnp.where(spot == at, 1.0, 0.0) for at in (main, upper, lower)]

    first = masks(0)
    others = masks(1)
    for k in range(2, kinds):
        others = [a + b for a, b in zip(others, masks(k))]
    picks = [jnp.concatenate([a, b], axis=0).astype(BF) for a, b in zip(first, others)]
    rows = nn(picks[0], got_ref[:, :width])
    tail = got_ref[:, width:]
    rows = rows + jnp.concatenate([nn(picks[1], tail), nn(picks[2], tail)], axis=1)
    query = (hidden_ref[...].astype(F32) + rows[:anchors]).astype(BF)
    positive = (rows[anchors:] / count_ref[...].astype(F32)).astype(BF)
    query_ref[...] = query
    positive_ref[...] = positive
    logit_ref[...] = jnp.sum(query.astype(F32) * positive.astype(F32), axis=1, keepdims=True) * scale


def unpack(got, place, hidden, count, scale):
    anchors, width = hidden.shape
    return pl.pallas_call(
        functools.partial(unpack_kernel, scale),
        out_shape=(
            jax.ShapeDtypeStruct((anchors, width), BF),
            jax.ShapeDtypeStruct((anchors, width), BF),
            jax.ShapeDtypeStruct((anchors, 1), F32),
        ),
        compiler_params=params(16),
        name="unpack",
    )(got, place, hidden, count)


def score_kernel(unit, near_ref, far_ref, *refs):
    pieces = (len(refs) - 4) // 2
    piece_refs, (logit_ref, level_ref, query_ref) = refs[:pieces], refs[pieces : pieces + 3]
    sent_refs, sems = refs[pieces + 3 : -1], refs[-1]
    step = pl.program_id(0)
    size = piece_refs[0].shape[0]
    copies = [
        pltpu.make_async_copy(ref, query_ref.at[pl.ds(k * size, size), :], sems.at[k])
        for k, ref in enumerate(piece_refs)
    ]

    @pl.when(step == 0)
    def _():
        for copy in copies:
            copy.start()

    for g in range(len(copies) // 2):

        @pl.when(step == g)
        def _():
            copies[2 * g].wait()
            copies[2 * g + 1].wait()

    queries = query_ref[pl.ds(pl.multiple_of(step * 2 * size, 2 * size), 2 * size), :]
    count = near_ref.shape[0]
    chunks = [(ref, row) for ref in (near_ref, far_ref) for row in range(0, count, CHUNK)]
    top = None
    for j, (ref, row) in enumerate(chunks):
        logits = lax.dot_general(
            ref[row : row + CHUNK, :], queries, (((1,), (1,)), ((), ())), preferred_element_type=F32
        )
        logit_ref[j * CHUNK : (j + 1) * CHUNK, :] = logits
        peak = jnp.max(logits, axis=0, keepdims=True)
        top = peak if top is None else jnp.maximum(top, peak)
    top = top * unit
    total, weights = 0.0, []
    for j in range(len(chunks)):
        one = jnp.exp2(logit_ref[j * CHUNK : (j + 1) * CHUNK, :] * unit - top)
        total = total + jnp.sum(one, axis=0, keepdims=True)
        weights.append(one.astype(BF))
    half = len(weights) // 2
    part = 0.0
    for ref, some in ((near_ref, weights[:half]), (far_ref, weights[half:])):
        turned = (((0,), (0,)), ((), ()))
        part = part + lax.dot_general(jnp.concatenate(some, axis=0), ref[...], turned, preferred_element_type=F32)
    level_ref[...] = top + jnp.log2(total)
    part, width = part.astype(BF), part.shape[1]
    blank = jnp.zeros((LABEL, width - size), F32)
    for g in range(pieces // 2):

        @pl.when(step == g)
        def _():
            for h in range(2):
                cut = slice(h * size, (h + 1) * size)
                label = split_rows(top[:, cut])
                sent_refs[2 * g + h][:size, :] = part[cut]
                sent_refs[2 * g + h][size:, :] = jnp.concatenate([label, blank], axis=1).astype(BF)


def split_rows(level):
    high = level.astype(BF).astype(F32)
    middle = (level - high).astype(BF).astype(F32)
    low = level - high - middle
    row = lax.broadcasted_iota(I32, (LABEL, level.shape[1]), 0)
    return jnp.where(row < 4, high, jnp.where(row < 8, middle, low))


def score(near, far, pieces, unit):
    cand_count, width = 2 * near.shape[0], near.shape[1]
    groups, each = len(pieces) // 2, 2 * pieces[0].shape[0]
    anchors = groups * each
    pairs = cand_count * anchors
    return pl.pallas_call(
        functools.partial(score_kernel, unit),
        grid=(groups,),
        in_specs=[pl.BlockSpec(near.shape, lambda i: (0, 0))] * 2
        + [pl.BlockSpec(memory_space=pl.ANY) for _ in pieces],
        out_specs=(
            pl.BlockSpec((cand_count, each), lambda i: (0, i)),
            pl.BlockSpec((1, each), lambda i: (0, i)),
            pl.BlockSpec((anchors, width), lambda i: (0, 0)),
        )
        + (pl.BlockSpec((each // 2 + LABEL, width), lambda i: (0, 0)),) * len(pieces),
        out_shape=(
            jax.ShapeDtypeStruct((cand_count, anchors), F32),
            jax.ShapeDtypeStruct((1, anchors), F32),
            jax.ShapeDtypeStruct((anchors, width), BF),
        )
        + (jax.ShapeDtypeStruct((each // 2 + LABEL, width), BF),) * len(pieces),
        scratch_shapes=[pltpu.SemaphoreType.DMA((len(pieces),))],
        compiler_params=params(56),
        cost_estimate=cost(4 * pairs * width, 4 * pairs, pairs),
        name="score",
    )(near, far, *pieces)


def cand_kernel(unit, *refs):
    arrays = (len(refs) - 2) // 2
    logit_refs, total_ref, query_refs, part_ref = refs[:arrays], refs[arrays], refs[arrays + 1 : -1], refs[-1]
    part, start = 0.0, 0
    for logit_ref, query_ref in zip(logit_refs, query_refs):
        stop = start + logit_ref.shape[1]
        weights = jnp.exp2(logit_ref[...] * unit - total_ref[:, start:stop]).astype(BF)
        part = part + nn(weights, query_ref[...])
        start = stop
    part_ref[...] = part.astype(part_ref.dtype)


def cand_terms(logits, total, queries, first, count, kind, unit):
    width = queries[0].shape[1]
    anchors = total.shape[1]
    start = first // TILE
    pairs = count * anchors
    return pl.pallas_call(
        functools.partial(cand_kernel, unit),
        grid=(count // TILE,),
        in_specs=[pl.BlockSpec((TILE, part.shape[1]), lambda i: (i + start, 0)) for part in logits]
        + [pl.BlockSpec((1, anchors), lambda i: (0, 0))]
        + [pl.BlockSpec(part.shape, lambda i: (0, 0)) for part in queries],
        out_specs=pl.BlockSpec((TILE, width), lambda i: (i, 0)),
        out_shape=jax.ShapeDtypeStruct((count, width), kind),
        compiler_params=params(60),
        cost_estimate=cost(2 * pairs * width, 4 * pairs, pairs),
        name="cand_terms",
    )(*logits, total, *queries)


def merge(levels):
    top = functools.reduce(jnp.maximum, levels)
    return top + jnp.log2(sum(jnp.exp2(level - top) for level in levels))


def table_kernel(*refs):
    level_refs, (logit_ref, table_ref) = refs[:-2], refs[-2:]
    levels = jnp.concatenate([ref[...] for ref in level_refs], axis=1)
    half = table_ref.shape[1] // 2
    size = 2 * SIDE * half
    levels = jnp.concatenate([levels[:, j * size : (j + 1) * size] for j in ORDER], axis=1)
    rows = []
    for x in range(SIDE):
        for z in range(SIDE):
            a_part = levels[:, x * size + z * half : x * size + (z + 1) * half]
            b_part = levels[:, z * size + (SIDE + x) * half : z * size + (SIDE + x + 1) * half]
            rows.append(jnp.concatenate([a_part, b_part], axis=1))
    rows[0] = merge([rows[0], logit_ref[...] * math.log2(math.e)])
    table_ref[...] = jnp.concatenate(rows, axis=0)


def table(levels, pos_logit, anchors):
    return pl.pallas_call(
        table_kernel,
        out_shape=jax.ShapeDtypeStruct((SIDE * SIDE, anchors), F32),
        compiler_params=params(8),
        name="level_table",
    )(*levels, pos_logit)


def rolled(value, along_x, by):
    if along_x:
        cut = (SIDE - by) * SIDE
        return jnp.concatenate([value[cut:], value[:cut]], axis=0)
    rows = []
    for x in range(SIDE):
        cut = x * SIDE + SIDE - by
        rows += [value[cut : (x + 1) * SIDE], value[x * SIDE : cut]]
    return jnp.concatenate(rows, axis=0)


def merge_kernel(along_x, own_ref, *refs):
    came_refs, out_ref = refs[:-1], refs[-1]
    levels = [own_ref[...]]
    for by, ref in zip((1, 2, 3), came_refs):
        levels.append(rolled(ref[...], along_x, by))
    out_ref[...] = merge(levels)


def merged(own, came, along_x):
    return pl.pallas_call(
        functools.partial(merge_kernel, along_x),
        out_shape=jax.ShapeDtypeStruct(own.shape, F32),
        compiler_params=params(8),
        name="level_merge",
    )(own, *came)


def spread_kernel(own_ref, *refs):
    came_refs, (total_ref, log_ref) = refs[:3], refs[3:]
    levels = [own_ref[...]]
    for by, ref in zip((1, 2, 3), came_refs):
        levels.append(rolled(ref[...], True, by))
    table = merge(levels)
    half = table.shape[1] // 2
    for j in range(SIDE):
        a_parts = [table[j * SIDE + i : j * SIDE + i + 1, :half] for i in range(SIDE)]
        b_parts = [table[i * SIDE + j : i * SIDE + j + 1, half:] for i in range(SIDE)]
        row = jnp.concatenate(a_parts + b_parts, axis=1)
        size, at = row.shape[1], ORDER[j]
        total_ref[:, at * size : (at + 1) * size] = row
    log_ref[...] = table[0:1] * math.log(2.0)


def spread(own, came):
    groups, anchors = own.shape
    return pl.pallas_call(
        spread_kernel,
        out_shape=(
            jax.ShapeDtypeStruct((1, groups * anchors), F32),
            jax.ShapeDtypeStruct((1, anchors), F32),
        ),
        compiler_params=params(8),
        name="level_spread",
    )(own, *came)


def combine_kernel(total_ref, *refs):
    piece_refs, out_refs = refs[: 2 * SIDE], refs[2 * SIDE :]
    rows = piece_refs[0].shape[0] - LABEL
    half = rows // SIDE
    for h in range(2):
        total = total_ref[:, h * rows : (h + 1) * rows]
        joined = 0.0
        for ref in piece_refs[h * SIDE : (h + 1) * SIDE]:
            label = ref[rows:, :rows].astype(F32)
            level = label[0:1] + label[4:5] + label[8:9]
            factor = jnp.broadcast_to(jnp.exp2(level - total), (8, rows)).T[:, :1]
            joined = joined + ref[:rows, :].astype(F32) * factor
        for d in range(SIDE):
            out_ref = out_refs[h * SIDE + d]
            out_ref[...] = joined[d * half : (d + 1) * half].astype(out_ref.dtype)


def combine(total, pieces):
    rows, width = pieces[0].shape
    half = (rows - LABEL) // SIDE
    one = tuple(jax.ShapeDtypeStruct((half, width), F32 if d == 0 else BF) for d in range(SIDE))
    return pl.pallas_call(
        combine_kernel,
        out_shape=one + one,
        compiler_params=params(40),
        name="combine",
    )(total, *pieces)


def body(anchor_hidden, candidates, memory, anchor_ids, pos_ids, pos_count, snapshot):
    anchors, width = anchor_hidden.shape
    scale = 1.0 / math.sqrt(width)
    unit = scale * math.log2(math.e)
    half = anchors // 2
    steps = (1, 2, 3)

    along_y = [shift_y(candidates, d) for d in steps]

    ids = jnp.concatenate([anchor_ids[:, None], pos_ids], axis=1)
    requests, place = plan(ids.T, ids)
    asked = lax.all_to_all(requests, ("row", "col"), split_axis=0, concat_axis=0, tiled=True)
    asked, *along_y = lax.optimization_barrier((asked, *along_y))
    along_y = jnp.concatenate([candidates] + along_y, axis=0)
    near, far = along_y, swap_core(along_y)
    served = serve(snapshot, asked, memory)
    devices = asked.shape[0]
    served = served.reshape(devices, MAIN, served.shape[1])
    got = lax.all_to_all(served, ("row", "col"), split_axis=0, concat_axis=0, tiled=True)
    got = got.reshape(devices * MAIN, got.shape[2])
    query, positive, pos_logit = unpack(got, place, anchor_hidden, pos_count[:, None], scale)
    pos_logit = pos_logit.reshape(anchors)

    first, second = query[:half], query[half:]
    first = jnp.concatenate([first] + [shift_z(first, d) for d in steps], axis=0)
    second = jnp.concatenate([second] + [shift_x(second, d) for d in steps], axis=0)
    first, second = lax.optimization_barrier((first, second))
    came = {d: [shift_x(first, d), shift_z(second, d)] for d in (1, 3)}
    own = score(near, far, [first, second], unit)
    own_level, first, second, *came_13 = lax.optimization_barrier((own[1], first, second, *came[1], *came[3]))
    far_pieces = [shift_x(first, 2), shift_z(second, 2)]
    sides = score(near, far, came_13, unit)
    side_level, *far_pieces = lax.optimization_barrier((sides[1], *far_pieces))
    last = score(near, far, far_pieces, unit)
    sent = {1: list(sides[3:5]), 3: list(sides[5:7]), 2: list(last[3:5])}
    own_a, own_b = own[3:]
    logits, queries = (own[0], sides[0], last[0]), (own[2], sides[2], last[2])
    levels = (own_level, side_level, last[1])

    known = table(levels, pos_logit.reshape(1, anchors), anchors)
    known = merged(known, [shift_z(known, d) for d in steps], False)
    total, log_total = spread(known, [shift_x(known, d) for d in steps])
    log_total = log_total.reshape(anchors)

    total, *sides = lax.optimization_barrier((total, *sent[1], *sent[3]))
    sent[1], sent[3] = sides[:2], sides[2:]
    a_came = {d: shift_x(sent[d][0], -d) for d in (1, 3)}
    b_came = {d: shift_z(sent[d][1], -d) for d in (1, 3)}
    count = near.shape[0]
    away = cand_terms(logits, total, queries, count, count, BF, unit)
    total, away = lax.optimization_barrier((total, away))
    came = swap_core(away).astype(F32)
    home = cand_terms(logits, total, queries, 0, count, F32, unit)
    _, a_came[1], b_came[1], a_came[3], b_came[3], *sent[2] = lax.optimization_barrier(
        (home, a_came[1], b_came[1], a_came[3], b_came[3], *sent[2])
    )
    a_came[2], b_came[2] = shift_x(sent[2][0], -2), shift_z(sent[2][1], -2)
    shard = candidates.shape[0]
    held = [home[d * shard : (d + 1) * shard] + came[d * shard : (d + 1) * shard] for d in range(SIDE)]
    moved = [shift_y(held[d].astype(BF), -d) for d in steps]
    total, moved[0] = lax.optimization_barrier((total, moved[0]))
    cand_grad = held[0]
    for one in moved:
        cand_grad = cand_grad + one.astype(F32)

    summed = combine(total, [own_a] + [a_came[d] for d in steps] + [own_b] + [b_came[d] for d in steps])
    a_all, b_all = summed[0], summed[SIDE]
    for d in steps:
        a_all = a_all + shift_z(summed[d], -d).astype(F32)
        b_all = b_all + shift_x(summed[SIDE + d], -d).astype(F32)
    weighted = jnp.concatenate([a_all, b_all], axis=0)
    anchor_grad = weighted + (jnp.exp(pos_logit - log_total) - 1.0)[:, None] * positive.astype(F32)
    loss = log_total - pos_logit

    return (loss, anchor_grad, cand_grad)


def solution(mesh):
    in_specs = (
        P(("row", "col"), None),
        P(("col", "row"), None),
        P(None, ("row", "col"), None),
        P(("row", "col")),
        P(("row", "col"), None),
        P(("row", "col")),
        P(),
    )
    out_specs = (P(("row", "col")), P(("row", "col"), None), P(("col", "row"), None))
    return jax.shard_map(body, mesh=mesh, in_specs=in_specs, out_specs=out_specs, check_vma=False)
```

```python
import functools
import math

import jax
import jax.numpy as jnp
from jax import lax
from jax.experimental import pallas as pl
from jax.experimental.pallas import tpu as pltpu
from jax.sharding import PartitionSpec as P

BF = jnp.bfloat16
F32 = jnp.float32
I32 = jnp.int32
SIDE = 4
MIB = 1024 * 1024
MAIN = 8
SPARE = 4
TILE = 512
CHUNK = 256
LABEL = 16
ORDER = (0, 1, 3, 2)


def params(mib):
    return pltpu.CompilerParams(vmem_limit_bytes=mib * MIB)


def cost(flops, moved, exps=0):
    return pl.CostEstimate(flops=1, bytes_accessed=1, transcendentals=0)


def nn(a, b):
    return jnp.dot(a, b, preferred_element_type=F32)


def shift_x(value, by):
    pairs = [(x * SIDE + z, (x + by) % SIDE * SIDE + z) for x in range(SIDE) for z in range(SIDE)]
    return lax.ppermute(value, "row", pairs)


def shift_z(value, by):
    pairs = [(x * SIDE + z, x * SIDE + (z + by) % SIDE) for x in range(SIDE) for z in range(SIDE)]
    return lax.ppermute(value, "row", pairs)


def shift_y(value, by):
    pairs = [(y * 2 + k, (y + by) % SIDE * 2 + k) for y in range(SIDE) for k in range(2)]
    return lax.ppermute(value, "col", pairs)


def swap_core(value):
    return lax.ppermute(value, "col", [(i, i ^ 1) for i in range(2 * SIDE)])


def plan_kernel(rows_ref, cols_ref, request_ref, place_ref):
    rows, cols = rows_ref[...], cols_ref[...]
    kinds, anchors = rows.shape
    total = kinds * anchors
    across = jnp.concatenate([rows[k : k + 1, :] for k in range(kinds)], axis=1)
    down = jnp.concatenate([cols[:, k : k + 1] for k in range(kinds)], axis=0)
    owner_across = jnp.where(across >= 0, across >> 10, -1)
    owner_down = jnp.where(down >= 0, down >> 10, -2)
    first = lax.broadcasted_iota(I32, (total, total), 0)
    second = lax.broadcasted_iota(I32, (total, total), 1)
    same = (owner_down == owner_across) & (second < first)
    slot = jnp.sum(jnp.where(same, 1.0, 0.0), axis=1, keepdims=True).astype(I32)
    kind = jnp.where(lax.broadcasted_iota(I32, (total, 1), 0) < anchors, 0, 1024)
    code = (down & 1023) + kind + 1
    hit = (slot == lax.broadcasted_iota(I32, (total, 128), 1)) & (down >= 0)
    low = jnp.where(hit, code & 63, 0).astype(F32).astype(BF)
    high = jnp.where(hit, code >> 6, 0).astype(F32).astype(BF)
    devices = request_ref.shape[0]
    pick = jnp.where(owner_across == lax.broadcasted_iota(I32, (devices, total), 0), 1.0, 0.0).astype(BF)
    found = nn(pick, low) + 64.0 * nn(pick, high) - 1.0
    request_ref[...] = found[:, : request_ref.shape[1]].astype(I32)
    place = jnp.where(down >= 0, owner_down * 16 + slot, -1)
    for k in range(kinds):
        place_ref[:, k : k + 1] = place[k * anchors : (k + 1) * anchors]


def plan(rows, cols):
    return pl.pallas_call(
        plan_kernel,
        out_shape=(jax.ShapeDtypeStruct((128, 16), I32), jax.ShapeDtypeStruct(cols.shape, I32)),
        compiler_params=params(16),
        name="plan",
    )(rows, cols)


def serve_kernel(asked_ref, memory_ref, out_ref):
    asked = asked_ref[...]
    devices, lanes = asked.shape
    nodes, width = memory_ref.shape[1:]

    def rows_of(first, slots):
        count = devices * slots
        wide = jnp.broadcast_to(asked[:, None, :], (devices, slots, lanes)).reshape(count, lanes)
        lane = lax.broadcasted_iota(I32, (count, lanes), 1)
        spot = lax.broadcasted_iota(I32, (count, lanes), 0) & (slots - 1)
        code = jnp.sum(jnp.where(lane == first + spot, wide, 0), axis=1, keepdims=True)
        node = lax.broadcasted_iota(I32, (count, nodes), 1)
        now = jnp.where(node == code, 1.0, 0.0).astype(BF)
        later = jnp.where(node + nodes == code, 1.0, 0.0).astype(BF)
        return (nn(now, memory_ref[0]) + nn(later, memory_ref[1])).astype(BF)

    out_ref[:, :width] = rows_of(0, MAIN)
    extra = rows_of(MAIN, SPARE)
    half = width // 2
    row = lax.broadcasted_iota(I32, (devices * MAIN, devices * SPARE), 0)
    column = lax.broadcasted_iota(I32, (devices * MAIN, devices * SPARE), 1)
    spot = row & (MAIN - 1)
    match = (row >> 3) * SPARE + (spot & (SPARE - 1)) == column
    upper = jnp.where(match & (spot < SPARE), 1.0, 0.0).astype(BF)
    lower = jnp.where(match & (spot >= SPARE), 1.0, 0.0).astype(BF)
    out_ref[:, width:] = (nn(upper, extra[:, :half]) + nn(lower, extra[:, half:])).astype(BF)


def serve(asked, memory):
    devices, lanes = asked.shape
    _, nodes, width = memory.shape
    step = 64
    return pl.pallas_call(
        serve_kernel,
        grid=(devices // step,),
        in_specs=[
            pl.BlockSpec((step, lanes), lambda i: (i, 0)),
            pl.BlockSpec(memory.shape, lambda i: (0, 0, 0)),
        ],
        out_specs=pl.BlockSpec((step * MAIN, width + width // 2), lambda i: (i, 0)),
        out_shape=jax.ShapeDtypeStruct((devices * MAIN, width + width // 2), BF),
        compiler_params=params(36),
        name="serve",
    )(asked, memory)


def unpack_kernel(scale, got_ref, place_ref, hidden_ref, count_ref, query_ref, positive_ref, logit_ref):
    anchors, kinds = place_ref.shape
    total, wide = got_ref.shape
    width = hidden_ref.shape[1]
    spot = lax.broadcasted_iota(I32, (anchors, total), 1)

    def masks(k):
        place = place_ref[:, k : k + 1]
        base, slot = (place >> 4) * MAIN, place & 15
        live = place >= 0
        main = jnp.where(live & (slot < MAIN), base + slot, -1)
        upper = jnp.where(live & (slot >= MAIN), base + slot - MAIN, -1)
        lower = jnp.where(live & (slot >= MAIN), base + slot - MAIN + SPARE, -1)
        return [jnp.where(spot == at, 1.0, 0.0) for at in (main, upper, lower)]

    first = masks(0)
    others = masks(1)
    for k in range(2, kinds):
        others = [a + b for a, b in zip(others, masks(k))]
    picks = [jnp.concatenate([a, b], axis=0).astype(BF) for a, b in zip(first, others)]
    rows = nn(picks[0], got_ref[:, :width])
    tail = got_ref[:, width:]
    rows = rows + jnp.concatenate([nn(picks[1], tail), nn(picks[2], tail)], axis=1)
    query = (hidden_ref[...].astype(F32) + rows[:anchors]).astype(BF)
    positive = (rows[anchors:] / count_ref[...].astype(F32)).astype(BF)
    query_ref[...] = query
    positive_ref[...] = positive
    logit_ref[...] = jnp.sum(query.astype(F32) * positive.astype(F32), axis=1, keepdims=True) * scale


def unpack(got, place, hidden, count, scale):
    anchors, width = hidden.shape
    return pl.pallas_call(
        functools.partial(unpack_kernel, scale),
        out_shape=(
            jax.ShapeDtypeStruct((anchors, width), BF),
            jax.ShapeDtypeStruct((anchors, width), BF),
            jax.ShapeDtypeStruct((anchors, 1), F32),
        ),
        compiler_params=params(16),
        name="unpack",
    )(got, place, hidden, count)


def score_kernel(unit, near_ref, far_ref, *refs):
    pieces = (len(refs) - 4) // 2
    piece_refs, (logit_ref, level_ref, query_ref) = refs[:pieces], refs[pieces : pieces + 3]
    sent_refs, sems = refs[pieces + 3 : -1], refs[-1]
    step = pl.program_id(0)
    size = piece_refs[0].shape[0]
    copies = [
        pltpu.make_async_copy(ref, query_ref.at[pl.ds(k * size, size), :], sems.at[k])
        for k, ref in enumerate(piece_refs)
    ]

    @pl.when(step == 0)
    def _():
        for copy in copies:
            copy.start()

    for g in range(len(copies) // 2):

        @pl.when(step == g)
        def _():
            copies[2 * g].wait()
            copies[2 * g + 1].wait()

    queries = query_ref[pl.ds(pl.multiple_of(step * 2 * size, 2 * size), 2 * size), :]
    count = near_ref.shape[0]
    chunks = [(ref, row) for ref in (near_ref, far_ref) for row in range(0, count, CHUNK)]
    top = None
    for j, (ref, row) in enumerate(chunks):
        logits = lax.dot_general(
            ref[row : row + CHUNK, :], queries, (((1,), (1,)), ((), ())), preferred_element_type=F32
        )
        logit_ref[j * CHUNK : (j + 1) * CHUNK, :] = logits
        peak = jnp.max(logits, axis=0, keepdims=True)
        top = peak if top is None else jnp.maximum(top, peak)
    top = top * unit
    total, weights = 0.0, []
    for j in range(len(chunks)):
        one = jnp.exp2(logit_ref[j * CHUNK : (j + 1) * CHUNK, :] * unit - top)
        total = total + jnp.sum(one, axis=0, keepdims=True)
        weights.append(one.astype(BF))
    half = len(weights) // 2
    part = 0.0
    for ref, some in ((near_ref, weights[:half]), (far_ref, weights[half:])):
        turned = (((0,), (0,)), ((), ()))
        part = part + lax.dot_general(jnp.concatenate(some, axis=0), ref[...], turned, preferred_element_type=F32)
    level_ref[...] = top + jnp.log2(total)
    part, width = part.astype(BF), part.shape[1]
    blank = jnp.zeros((LABEL, width - size), F32)
    for g in range(pieces // 2):

        @pl.when(step == g)
        def _():
            for h in range(2):
                cut = slice(h * size, (h + 1) * size)
                label = split_rows(top[:, cut])
                sent_refs[2 * g + h][:size, :] = part[cut]
                sent_refs[2 * g + h][size:, :] = jnp.concatenate([label, blank], axis=1).astype(BF)


def split_rows(level):
    high = level.astype(BF).astype(F32)
    middle = (level - high).astype(BF).astype(F32)
    low = level - high - middle
    row = lax.broadcasted_iota(I32, (LABEL, level.shape[1]), 0)
    return jnp.where(row < 4, high, jnp.where(row < 8, middle, low))


def score(near, far, pieces, unit):
    cand_count, width = 2 * near.shape[0], near.shape[1]
    groups, each = len(pieces) // 2, 2 * pieces[0].shape[0]
    anchors = groups * each
    pairs = cand_count * anchors
    return pl.pallas_call(
        functools.partial(score_kernel, unit),
        grid=(groups,),
        in_specs=[pl.BlockSpec(near.shape, lambda i: (0, 0))] * 2
        + [pl.BlockSpec(memory_space=pl.ANY) for _ in pieces],
        out_specs=(
            pl.BlockSpec((cand_count, each), lambda i: (0, i)),
            pl.BlockSpec((1, each), lambda i: (0, i)),
            pl.BlockSpec((anchors, width), lambda i: (0, 0)),
        )
        + (pl.BlockSpec((each // 2 + LABEL, width), lambda i: (0, 0)),) * len(pieces),
        out_shape=(
            jax.ShapeDtypeStruct((cand_count, anchors), F32),
            jax.ShapeDtypeStruct((1, anchors), F32),
            jax.ShapeDtypeStruct((anchors, width), BF),
        )
        + (jax.ShapeDtypeStruct((each // 2 + LABEL, width), BF),) * len(pieces),
        scratch_shapes=[pltpu.SemaphoreType.DMA((len(pieces),))],
        compiler_params=params(56),
        cost_estimate=cost(4 * pairs * width, 4 * pairs, pairs),
        name="score",
    )(near, far, *pieces)


def cand_kernel(unit, *refs):
    arrays = (len(refs) - 2) // 2
    logit_refs, total_ref, query_refs, part_ref = refs[:arrays], refs[arrays], refs[arrays + 1 : -1], refs[-1]
    part, start = 0.0, 0
    for logit_ref, query_ref in zip(logit_refs, query_refs):
        stop = start + logit_ref.shape[1]
        weights = jnp.exp2(logit_ref[...] * unit - total_ref[:, start:stop]).astype(BF)
        part = part + nn(weights, query_ref[...])
        start = stop
    part_ref[...] = part.astype(part_ref.dtype)


def cand_terms(logits, total, queries, first, count, kind, unit):
    width = queries[0].shape[1]
    anchors = total.shape[1]
    start = first // TILE
    pairs = count * anchors
    return pl.pallas_call(
        functools.partial(cand_kernel, unit),
        grid=(count // TILE,),
        in_specs=[pl.BlockSpec((TILE, part.shape[1]), lambda i: (i + start, 0)) for part in logits]
        + [pl.BlockSpec((1, anchors), lambda i: (0, 0))]
        + [pl.BlockSpec(part.shape, lambda i: (0, 0)) for part in queries],
        out_specs=pl.BlockSpec((TILE, width), lambda i: (i, 0)),
        out_shape=jax.ShapeDtypeStruct((count, width), kind),
        compiler_params=params(60),
        cost_estimate=cost(2 * pairs * width, 4 * pairs, pairs),
        name="cand_terms",
    )(*logits, total, *queries)


def home_kernel(unit, *refs):
    arrays = (len(refs) - 6) // 2
    logit_refs, total_ref, query_refs = refs[:arrays], refs[arrays], refs[arrays + 1 : -5]
    came_ref, out_refs = refs[-5], refs[-4:]
    part, start = came_ref[...].astype(F32), 0
    for logit_ref, query_ref in zip(logit_refs, query_refs):
        stop = start + logit_ref.shape[1]
        weights = jnp.exp2(logit_ref[...] * unit - total_ref[:, start:stop]).astype(BF)
        part = part + nn(weights, query_ref[...])
        start = stop
    shard = out_refs[0].shape[0]
    each = part.shape[0] // shard
    for d, out_ref in enumerate(out_refs):

        @pl.when(pl.program_id(0) == d // each)
        def _():
            row = d % each * shard
            out_ref[...] = part[row : row + shard].astype(out_ref.dtype)


def home_terms(logits, total, queries, came, unit):
    count, width = came.shape
    anchors = total.shape[1]
    return pl.pallas_call(
        functools.partial(home_kernel, unit),
        grid=(count // TILE,),
        in_specs=[pl.BlockSpec((TILE, part.shape[1]), lambda i: (i, 0)) for part in logits]
        + [pl.BlockSpec((1, anchors), lambda i: (0, 0))]
        + [pl.BlockSpec(part.shape, lambda i: (0, 0)) for part in queries]
        + [pl.BlockSpec((TILE, width), lambda i: (i, 0))],
        out_specs=(pl.BlockSpec((count // SIDE, width), lambda i: (0, 0)),) * SIDE,
        out_shape=tuple(jax.ShapeDtypeStruct((count // SIDE, width), F32 if d == 0 else BF) for d in range(SIDE)),
        compiler_params=params(60),
        cost_estimate=cost(1, 1),
        name="home_terms",
    )(*logits, total, *queries, came)


def merge(levels):
    top = functools.reduce(jnp.maximum, levels)
    return top + jnp.log2(sum(jnp.exp2(level - top) for level in levels))


def table_kernel(*refs):
    level_refs, (logit_ref, table_ref) = refs[:-2], refs[-2:]
    levels = jnp.concatenate([ref[...] for ref in level_refs], axis=1)
    half = table_ref.shape[1] // 2
    size = 2 * SIDE * half
    levels = jnp.concatenate([levels[:, j * size : (j + 1) * size] for j in ORDER], axis=1)
    rows = []
    for x in range(SIDE):
        for z in range(SIDE):
            a_part = levels[:, x * size + z * half : x * size + (z + 1) * half]
            b_part = levels[:, z * size + (SIDE + x) * half : z * size + (SIDE + x + 1) * half]
            rows.append(jnp.concatenate([a_part, b_part], axis=1))
    rows[0] = merge([rows[0], logit_ref[...] * math.log2(math.e)])
    table_ref[...] = jnp.concatenate(rows, axis=0)


def table(levels, pos_logit, anchors):
    return pl.pallas_call(
        table_kernel,
        out_shape=jax.ShapeDtypeStruct((SIDE * SIDE, anchors), F32),
        compiler_params=params(8),
        name="level_table",
    )(*levels, pos_logit)


def rolled(value, along_x, by):
    if along_x:
        cut = (SIDE - by) * SIDE
        return jnp.concatenate([value[cut:], value[:cut]], axis=0)
    rows = []
    for x in range(SIDE):
        cut = x * SIDE + SIDE - by
        rows += [value[cut : (x + 1) * SIDE], value[x * SIDE : cut]]
    return jnp.concatenate(rows, axis=0)


def merge_kernel(along_x, own_ref, *refs):
    came_refs, out_ref = refs[:-1], refs[-1]
    levels = [own_ref[...]]
    for by, ref in zip((1, 2, 3), came_refs):
        levels.append(rolled(ref[...], along_x, by))
    out_ref[...] = merge(levels)


def merged(own, came, along_x):
    return pl.pallas_call(
        functools.partial(merge_kernel, along_x),
        out_shape=jax.ShapeDtypeStruct(own.shape, F32),
        compiler_params=params(8),
        name="level_merge",
    )(own, *came)


def spread_kernel(own_ref, *refs):
    came_refs, (total_ref, log_ref) = refs[:3], refs[3:]
    levels = [own_ref[...]]
    for by, ref in zip((1, 2, 3), came_refs):
        levels.append(rolled(ref[...], True, by))
    table = merge(levels)
    half = table.shape[1] // 2
    for j in range(SIDE):
        a_parts = [table[j * SIDE + i : j * SIDE + i + 1, :half] for i in range(SIDE)]
        b_parts = [table[i * SIDE + j : i * SIDE + j + 1, half:] for i in range(SIDE)]
        row = jnp.concatenate(a_parts + b_parts, axis=1)
        size, at = row.shape[1], ORDER[j]
        total_ref[:, at * size : (at + 1) * size] = row
    log_ref[...] = table[0:1] * math.log(2.0)


def spread(own, came):
    groups, anchors = own.shape
    return pl.pallas_call(
        spread_kernel,
        out_shape=(
            jax.ShapeDtypeStruct((1, groups * anchors), F32),
            jax.ShapeDtypeStruct((1, anchors), F32),
        ),
        compiler_params=params(8),
        name="level_spread",
    )(own, *came)


def combine_kernel(total_ref, *refs):
    piece_refs, out_refs = refs[: 2 * SIDE], refs[2 * SIDE :]
    rows = piece_refs[0].shape[0] - LABEL
    half = rows // SIDE
    for h in range(2):
        total = total_ref[:, h * rows : (h + 1) * rows]
        joined = 0.0
        for ref in piece_refs[h * SIDE : (h + 1) * SIDE]:
            label = ref[rows:, :rows].astype(F32)
            level = label[0:1] + label[4:5] + label[8:9]
            factor = jnp.broadcast_to(jnp.exp2(level - total), (8, rows)).T[:, :1]
            joined = joined + ref[:rows, :].astype(F32) * factor
        for d in range(SIDE):
            out_ref = out_refs[h * SIDE + d]
            out_ref[...] = joined[d * half : (d + 1) * half].astype(out_ref.dtype)


def combine(total, pieces):
    rows, width = pieces[0].shape
    half = (rows - LABEL) // SIDE
    one = tuple(jax.ShapeDtypeStruct((half, width), F32 if d == 0 else BF) for d in range(SIDE))
    return pl.pallas_call(
        combine_kernel,
        out_shape=one + one,
        compiler_params=params(40),
        name="combine",
    )(total, *pieces)


def body(anchor_hidden, candidates, memory, anchor_ids, pos_ids, pos_count, snapshot):
    anchors, width = anchor_hidden.shape
    scale = 1.0 / math.sqrt(width)
    unit = scale * math.log2(math.e)
    half = anchors // 2
    steps = (1, 2, 3)

    along_y = [shift_y(candidates, d) for d in steps]

    ids = jnp.concatenate([anchor_ids[:, None], pos_ids], axis=1)
    requests, place = plan(ids.T, ids)
    asked = lax.all_to_all(requests, ("row", "col"), split_axis=0, concat_axis=0, tiled=True)
    asked, *along_y = lax.optimization_barrier((asked, *along_y))
    along_y = jnp.concatenate([candidates] + along_y, axis=0)
    near, far = along_y, swap_core(along_y)
    served = serve(asked, lax.dynamic_slice_in_dim(memory, snapshot[0], 2, 0))
    devices = asked.shape[0]
    served = served.reshape(devices, MAIN, served.shape[1])
    got = lax.all_to_all(served, ("row", "col"), split_axis=0, concat_axis=0, tiled=True)
    got = got.reshape(devices * MAIN, got.shape[2])
    query, positive, pos_logit = unpack(got, place, anchor_hidden, pos_count[:, None], scale)
    pos_logit = pos_logit.reshape(anchors)

    first, second = query[:half], query[half:]
    first = jnp.concatenate([first] + [shift_z(first, d) for d in steps], axis=0)
    second = jnp.concatenate([second] + [shift_x(second, d) for d in steps], axis=0)
    first, second = lax.optimization_barrier((first, second))
    came = {d: [shift_x(first, d), shift_z(second, d)] for d in (1, 3)}
    own = score(near, far, [first, second], unit)
    own_level, first, second, *came_13 = lax.optimization_barrier((own[1], first, second, *came[1], *came[3]))
    far_pieces = [shift_x(first, 2), shift_z(second, 2)]
    sides = score(near, far, came_13, unit)
    side_level, *far_pieces = lax.optimization_barrier((sides[1], *far_pieces))
    last = score(near, far, far_pieces, unit)
    sent = {1: list(sides[3:5]), 3: list(sides[5:7]), 2: list(last[3:5])}
    own_a, own_b = own[3:]
    logits, queries = (own[0], sides[0], last[0]), (own[2], sides[2], last[2])
    levels = (own_level, side_level, last[1])

    known = table(levels, pos_logit.reshape(1, anchors), anchors)
    known = merged(known, [shift_z(known, d) for d in steps], False)
    total, log_total = spread(known, [shift_x(known, d) for d in steps])
    log_total = log_total.reshape(anchors)

    total, *sides = lax.optimization_barrier((total, *sent[1], *sent[3]))
    sent[1], sent[3] = sides[:2], sides[2:]
    a_came = {d: shift_x(sent[d][0], -d) for d in (1, 3)}
    b_came = {d: shift_z(sent[d][1], -d) for d in (1, 3)}
    count = near.shape[0]
    away = cand_terms(logits, total, queries, count, count, BF, unit)
    total, away = lax.optimization_barrier((total, away))
    came = swap_core(away)
    home = home_terms(logits, total, queries, came, unit)
    _, a_came[1], b_came[1], a_came[3], b_came[3], *sent[2] = lax.optimization_barrier(
        (home[0], a_came[1], b_came[1], a_came[3], b_came[3], *sent[2])
    )
    a_came[2], b_came[2] = shift_x(sent[2][0], -2), shift_z(sent[2][1], -2)
    moved = [shift_y(home[d], -d) for d in steps]
    total, moved[0] = lax.optimization_barrier((total, moved[0]))
    cand_grad = home[0]
    for one in moved:
        cand_grad = cand_grad + one.astype(F32)

    summed = combine(total, [own_a] + [a_came[d] for d in steps] + [own_b] + [b_came[d] for d in steps])
    a_all, b_all = summed[0], summed[SIDE]
    for d in steps:
        a_all = a_all + shift_z(summed[d], -d).astype(F32)
        b_all = b_all + shift_x(summed[SIDE + d], -d).astype(F32)
    weighted = jnp.concatenate([a_all, b_all], axis=0)
    anchor_grad = weighted + (jnp.exp(pos_logit - log_total) - 1.0)[:, None] * positive.astype(F32)
    loss = log_total - pos_logit

    return (loss, anchor_grad, cand_grad)


def solution(mesh):
    in_specs = (
        P(("row", "col"), None),
        P(("col", "row"), None),
        P(None, ("row", "col"), None),
        P(("row", "col")),
        P(("row", "col"), None),
        P(("row", "col")),
        P(),
    )
    out_specs = (P(("row", "col")), P(("row", "col"), None), P(("col", "row"), None))
    return jax.shard_map(body, mesh=mesh, in_specs=in_specs, out_specs=out_specs, check_vma=False)
```

```python
import functools
import math

import jax
import jax.numpy as jnp
from jax import lax
from jax.experimental import pallas as pl
from jax.experimental.pallas import tpu as pltpu
from jax.sharding import PartitionSpec as P

BF = jnp.bfloat16
F32 = jnp.float32
I32 = jnp.int32
SIDE = 4
MIB = 1024 * 1024
MAIN = 8
SPARE = 4
TILE = 512
CHUNK = 256
LABEL = 16
ORDER = (0, 1, 3, 2)


def params(mib):
    return pltpu.CompilerParams(vmem_limit_bytes=mib * MIB)


def cost(flops, moved, exps=0):
    return pl.CostEstimate(flops=1, bytes_accessed=1, transcendentals=0)


def nn(a, b):
    return jnp.dot(a, b, preferred_element_type=F32)


def shift_x(value, by):
    pairs = [(x * SIDE + z, (x + by) % SIDE * SIDE + z) for x in range(SIDE) for z in range(SIDE)]
    return lax.ppermute(value, "row", pairs)


def shift_z(value, by):
    pairs = [(x * SIDE + z, x * SIDE + (z + by) % SIDE) for x in range(SIDE) for z in range(SIDE)]
    return lax.ppermute(value, "row", pairs)


def shift_y(value, by):
    pairs = [(y * 2 + k, (y + by) % SIDE * 2 + k) for y in range(SIDE) for k in range(2)]
    return lax.ppermute(value, "col", pairs)


def swap_core(value):
    return lax.ppermute(value, "col", [(i, i ^ 1) for i in range(2 * SIDE)])


def plan_kernel(rows_ref, cols_ref, request_ref, place_ref):
    rows, cols = rows_ref[...], cols_ref[...]
    kinds, anchors = rows.shape
    total = kinds * anchors
    across = jnp.concatenate([rows[k : k + 1, :] for k in range(kinds)], axis=1)
    down = jnp.concatenate([cols[:, k : k + 1] for k in range(kinds)], axis=0)
    owner_across = jnp.where(across >= 0, across >> 10, -1)
    owner_down = jnp.where(down >= 0, down >> 10, -2)
    first = lax.broadcasted_iota(I32, (total, total), 0)
    second = lax.broadcasted_iota(I32, (total, total), 1)
    same = (owner_down == owner_across) & (second < first)
    slot = jnp.sum(jnp.where(same, 1.0, 0.0), axis=1, keepdims=True).astype(I32)
    kind = jnp.where(lax.broadcasted_iota(I32, (total, 1), 0) < anchors, 0, 1024)
    code = (down & 1023) + kind + 1
    hit = (slot == lax.broadcasted_iota(I32, (total, 128), 1)) & (down >= 0)
    low = jnp.where(hit, code & 63, 0).astype(F32).astype(BF)
    high = jnp.where(hit, code >> 6, 0).astype(F32).astype(BF)
    devices = request_ref.shape[0]
    pick = jnp.where(owner_across == lax.broadcasted_iota(I32, (devices, total), 0), 1.0, 0.0).astype(BF)
    found = nn(pick, low) + 64.0 * nn(pick, high) - 1.0
    request_ref[...] = found[:, : request_ref.shape[1]].astype(I32)
    place = jnp.where(down >= 0, owner_down * 16 + slot, -1)
    for k in range(kinds):
        place_ref[:, k : k + 1] = place[k * anchors : (k + 1) * anchors]


def plan(rows, cols):
    return pl.pallas_call(
        plan_kernel,
        out_shape=(jax.ShapeDtypeStruct((128, 16), I32), jax.ShapeDtypeStruct(cols.shape, I32)),
        compiler_params=params(16),
        name="plan",
    )(rows, cols)


def serve_kernel(asked_ref, memory_ref, out_ref):
    asked = asked_ref[...]
    devices, lanes = asked.shape
    nodes, width = memory_ref.shape[1:]

    def rows_of(first, slots):
        count = devices * slots
        wide = jnp.broadcast_to(asked[:, None, :], (devices, slots, lanes)).reshape(count, lanes)
        lane = lax.broadcasted_iota(I32, (count, lanes), 1)
        spot = lax.broadcasted_iota(I32, (count, lanes), 0) & (slots - 1)
        code = jnp.sum(jnp.where(lane == first + spot, wide, 0), axis=1, keepdims=True)
        node = lax.broadcasted_iota(I32, (count, nodes), 1)
        now = jnp.where(node == code, 1.0, 0.0).astype(BF)
        later = jnp.where(node + nodes == code, 1.0, 0.0).astype(BF)
        return (nn(now, memory_ref[0]) + nn(later, memory_ref[1])).astype(BF)

    out_ref[:, :width] = rows_of(0, MAIN)
    extra = rows_of(MAIN, SPARE)
    half = width // 2
    row = lax.broadcasted_iota(I32, (devices * MAIN, devices * SPARE), 0)
    column = lax.broadcasted_iota(I32, (devices * MAIN, devices * SPARE), 1)
    spot = row & (MAIN - 1)
    match = (row >> 3) * SPARE + (spot & (SPARE - 1)) == column
    upper = jnp.where(match & (spot < SPARE), 1.0, 0.0).astype(BF)
    lower = jnp.where(match & (spot >= SPARE), 1.0, 0.0).astype(BF)
    out_ref[:, width:] = (nn(upper, extra[:, :half]) + nn(lower, extra[:, half:])).astype(BF)


def serve(asked, memory):
    devices, lanes = asked.shape
    _, nodes, width = memory.shape
    step = 64
    return pl.pallas_call(
        serve_kernel,
        grid=(devices // step,),
        in_specs=[
            pl.BlockSpec((step, lanes), lambda i: (i, 0)),
            pl.BlockSpec(memory.shape, lambda i: (0, 0, 0)),
        ],
        out_specs=pl.BlockSpec((step * MAIN, width + width // 2), lambda i: (i, 0)),
        out_shape=jax.ShapeDtypeStruct((devices * MAIN, width + width // 2), BF),
        compiler_params=params(36),
        name="serve",
    )(asked, memory)


def unpack_kernel(scale, got_ref, place_ref, hidden_ref, count_ref, query_ref, positive_ref, logit_ref):
    anchors, kinds = place_ref.shape
    total, wide = got_ref.shape
    width = hidden_ref.shape[1]
    spot = lax.broadcasted_iota(I32, (anchors, total), 1)

    def masks(k):
        place = place_ref[:, k : k + 1]
        base, slot = (place >> 4) * MAIN, place & 15
        live = place >= 0
        main = jnp.where(live & (slot < MAIN), base + slot, -1)
        upper = jnp.where(live & (slot >= MAIN), base + slot - MAIN, -1)
        lower = jnp.where(live & (slot >= MAIN), base + slot - MAIN + SPARE, -1)
        return [jnp.where(spot == at, 1.0, 0.0) for at in (main, upper, lower)]

    first = masks(0)
    others = masks(1)
    for k in range(2, kinds):
        others = [a + b for a, b in zip(others, masks(k))]
    picks = [jnp.concatenate([a, b], axis=0).astype(BF) for a, b in zip(first, others)]
    rows = nn(picks[0], got_ref[:, :width])
    tail = got_ref[:, width:]
    rows = rows + jnp.concatenate([nn(picks[1], tail), nn(picks[2], tail)], axis=1)
    query = (hidden_ref[...].astype(F32) + rows[:anchors]).astype(BF)
    positive = (rows[anchors:] / count_ref[...].astype(F32)).astype(BF)
    query_ref[...] = query
    positive_ref[...] = positive
    logit_ref[...] = jnp.sum(query.astype(F32) * positive.astype(F32), axis=1, keepdims=True) * scale


def unpack(got, place, hidden, count, scale):
    anchors, width = hidden.shape
    return pl.pallas_call(
        functools.partial(unpack_kernel, scale),
        out_shape=(
            jax.ShapeDtypeStruct((anchors, width), BF),
            jax.ShapeDtypeStruct((anchors, width), BF),
            jax.ShapeDtypeStruct((anchors, 1), F32),
        ),
        compiler_params=params(16),
        name="unpack",
    )(got, place, hidden, count)


def score_kernel(unit, near_ref, far_ref, *refs):
    pieces = (len(refs) - 4) // 2
    piece_refs, (logit_ref, level_ref, query_ref) = refs[:pieces], refs[pieces : pieces + 3]
    sent_refs, sems = refs[pieces + 3 : -1], refs[-1]
    step = pl.program_id(0)
    size = piece_refs[0].shape[0]
    copies = [
        pltpu.make_async_copy(ref, query_ref.at[pl.ds(k * size, size), :], sems.at[k])
        for k, ref in enumerate(piece_refs)
    ]

    @pl.when(step == 0)
    def _():
        for copy in copies:
            copy.start()

    for g in range(len(copies) // 2):

        @pl.when(step == g)
        def _():
            copies[2 * g].wait()
            copies[2 * g + 1].wait()

    queries = query_ref[pl.ds(pl.multiple_of(step * 2 * size, 2 * size), 2 * size), :]
    count = near_ref.shape[0]
    chunks = [(ref, row) for ref in (near_ref, far_ref) for row in range(0, count, CHUNK)]
    top = None
    for j, (ref, row) in enumerate(chunks):
        logits = lax.dot_general(
            ref[row : row + CHUNK, :], queries, (((1,), (1,)), ((), ())), preferred_element_type=F32
        )
        logit_ref[j * CHUNK : (j + 1) * CHUNK, :] = logits
        peak = jnp.max(logits, axis=0, keepdims=True)
        top = peak if top is None else jnp.maximum(top, peak)
    top = top * unit
    total, weights = 0.0, []
    for j in range(len(chunks)):
        one = jnp.exp2(logit_ref[j * CHUNK : (j + 1) * CHUNK, :] * unit - top)
        total = total + jnp.sum(one, axis=0, keepdims=True)
        weights.append(one.astype(BF))
    half = len(weights) // 2
    part = 0.0
    for ref, some in ((near_ref, weights[:half]), (far_ref, weights[half:])):
        turned = (((0,), (0,)), ((), ()))
        part = part + lax.dot_general(jnp.concatenate(some, axis=0), ref[...], turned, preferred_element_type=F32)
    level_ref[...] = top + jnp.log2(total)
    part, width = part.astype(BF), part.shape[1]
    blank = jnp.zeros((LABEL, width - size), F32)
    for g in range(pieces // 2):

        @pl.when(step == g)
        def _():
            for h in range(2):
                cut = slice(h * size, (h + 1) * size)
                label = split_rows(top[:, cut])
                sent_refs[2 * g + h][:size, :] = part[cut]
                sent_refs[2 * g + h][size:, :] = jnp.concatenate([label, blank], axis=1).astype(BF)


def split_rows(level):
    high = level.astype(BF).astype(F32)
    middle = (level - high).astype(BF).astype(F32)
    low = level - high - middle
    row = lax.broadcasted_iota(I32, (LABEL, level.shape[1]), 0)
    return jnp.where(row < 4, high, jnp.where(row < 8, middle, low))


def score(near, far, pieces, unit):
    cand_count, width = 2 * near.shape[0], near.shape[1]
    groups, each = len(pieces) // 2, 2 * pieces[0].shape[0]
    anchors = groups * each
    pairs = cand_count * anchors
    return pl.pallas_call(
        functools.partial(score_kernel, unit),
        grid=(groups,),
        in_specs=[pl.BlockSpec(near.shape, lambda i: (0, 0))] * 2
        + [pl.BlockSpec(memory_space=pl.ANY) for _ in pieces],
        out_specs=(
            pl.BlockSpec((cand_count, each), lambda i: (0, i)),
            pl.BlockSpec((1, each), lambda i: (0, i)),
            pl.BlockSpec((anchors, width), lambda i: (0, 0)),
        )
        + (pl.BlockSpec((each // 2 + LABEL, width), lambda i: (0, 0)),) * len(pieces),
        out_shape=(
            jax.ShapeDtypeStruct((cand_count, anchors), F32),
            jax.ShapeDtypeStruct((1, anchors), F32),
            jax.ShapeDtypeStruct((anchors, width), BF),
        )
        + (jax.ShapeDtypeStruct((each // 2 + LABEL, width), BF),) * len(pieces),
        scratch_shapes=[pltpu.SemaphoreType.DMA((len(pieces),))],
        compiler_params=params(56),
        cost_estimate=cost(4 * pairs * width, 4 * pairs, pairs),
        name="score",
    )(near, far, *pieces)


def cand_kernel(unit, *refs):
    arrays = (len(refs) - 2) // 2
    logit_refs, total_ref, query_refs, part_ref = refs[:arrays], refs[arrays], refs[arrays + 1 : -1], refs[-1]
    part, start = 0.0, 0
    for logit_ref, query_ref in zip(logit_refs, query_refs):
        stop = start + logit_ref.shape[1]
        weights = jnp.exp2(logit_ref[...] * unit - total_ref[:, start:stop]).astype(BF)
        part = part + nn(weights, query_ref[...])
        start = stop
    part_ref[...] = part.astype(part_ref.dtype)


def cand_terms(logits, total, queries, first, count, kind, unit):
    width = queries[0].shape[1]
    anchors = total.shape[1]
    start = first // TILE
    pairs = count * anchors
    return pl.pallas_call(
        functools.partial(cand_kernel, unit),
        grid=(count // TILE,),
        in_specs=[pl.BlockSpec((TILE, part.shape[1]), lambda i: (i + start, 0)) for part in logits]
        + [pl.BlockSpec((1, anchors), lambda i: (0, 0))]
        + [pl.BlockSpec(part.shape, lambda i: (0, 0)) for part in queries],
        out_specs=pl.BlockSpec((TILE, width), lambda i: (i, 0)),
        out_shape=jax.ShapeDtypeStruct((count, width), kind),
        compiler_params=params(60),
        cost_estimate=cost(2 * pairs * width, 4 * pairs, pairs),
        name="cand_terms",
    )(*logits, total, *queries)


def home_kernel(unit, *refs):
    arrays = (len(refs) - 6) // 2
    logit_refs, total_ref, query_refs = refs[:arrays], refs[arrays], refs[arrays + 1 : -5]
    came_ref, out_refs = refs[-5], refs[-4:]
    part, start = came_ref[...].astype(F32), 0
    for logit_ref, query_ref in zip(logit_refs, query_refs):
        stop = start + logit_ref.shape[1]
        weights = jnp.exp2(logit_ref[...] * unit - total_ref[:, start:stop]).astype(BF)
        part = part + nn(weights, query_ref[...])
        start = stop
    shard = out_refs[0].shape[0]
    each = part.shape[0] // shard
    for d, out_ref in enumerate(out_refs):

        @pl.when(pl.program_id(0) == d // each)
        def _():
            row = d % each * shard
            out_ref[...] = part[row : row + shard].astype(out_ref.dtype)


def home_terms(logits, total, queries, came, unit):
    count, width = came.shape
    anchors = total.shape[1]
    return pl.pallas_call(
        functools.partial(home_kernel, unit),
        grid=(count // TILE,),
        in_specs=[pl.BlockSpec((TILE, part.shape[1]), lambda i: (i, 0)) for part in logits]
        + [pl.BlockSpec((1, anchors), lambda i: (0, 0))]
        + [pl.BlockSpec(part.shape, lambda i: (0, 0)) for part in queries]
        + [pl.BlockSpec((TILE, width), lambda i: (i, 0))],
        out_specs=(pl.BlockSpec((count // SIDE, width), lambda i: (0, 0)),) * SIDE,
        out_shape=tuple(jax.ShapeDtypeStruct((count // SIDE, width), F32 if d == 0 else BF) for d in range(SIDE)),
        compiler_params=params(60),
        cost_estimate=cost(1, 1),
        name="home_terms",
    )(*logits, total, *queries, came)


def merge(levels):
    top = functools.reduce(jnp.maximum, levels)
    return top + jnp.log2(sum(jnp.exp2(level - top) for level in levels))


def table_kernel(*refs):
    level_refs, (logit_ref, table_ref) = refs[:-2], refs[-2:]
    levels = jnp.concatenate([ref[...] for ref in level_refs], axis=1)
    half = table_ref.shape[1] // 2
    size = 2 * SIDE * half
    levels = jnp.concatenate([levels[:, j * size : (j + 1) * size] for j in ORDER], axis=1)
    rows = []
    for x in range(SIDE):
        for z in range(SIDE):
            a_part = levels[:, x * size + z * half : x * size + (z + 1) * half]
            b_part = levels[:, z * size + (SIDE + x) * half : z * size + (SIDE + x + 1) * half]
            rows.append(jnp.concatenate([a_part, b_part], axis=1))
    rows[0] = merge([rows[0], logit_ref[...] * math.log2(math.e)])
    table_ref[...] = jnp.concatenate(rows, axis=0)


def table(levels, pos_logit, anchors):
    return pl.pallas_call(
        table_kernel,
        out_shape=jax.ShapeDtypeStruct((SIDE * SIDE, anchors), F32),
        compiler_params=params(8),
        name="level_table",
    )(*levels, pos_logit)


def rolled(value, along_x, by):
    if along_x:
        cut = (SIDE - by) * SIDE
        return jnp.concatenate([value[cut:], value[:cut]], axis=0)
    rows = []
    for x in range(SIDE):
        cut = x * SIDE + SIDE - by
        rows += [value[cut : (x + 1) * SIDE], value[x * SIDE : cut]]
    return jnp.concatenate(rows, axis=0)


def merge_kernel(along_x, own_ref, *refs):
    came_refs, out_ref = refs[:-1], refs[-1]
    levels = [own_ref[...]]
    for by, ref in zip((1, 2, 3), came_refs):
        levels.append(rolled(ref[...], along_x, by))
    out_ref[...] = merge(levels)


def merged(own, came, along_x):
    return pl.pallas_call(
        functools.partial(merge_kernel, along_x),
        out_shape=jax.ShapeDtypeStruct(own.shape, F32),
        compiler_params=params(8),
        name="level_merge",
    )(own, *came)


def spread_kernel(own_ref, *refs):
    came_refs, (total_ref, log_ref) = refs[:3], refs[3:]
    levels = [own_ref[...]]
    for by, ref in zip((1, 2, 3), came_refs):
        levels.append(rolled(ref[...], True, by))
    table = merge(levels)
    half = table.shape[1] // 2
    for j in range(SIDE):
        a_parts = [table[j * SIDE + i : j * SIDE + i + 1, :half] for i in range(SIDE)]
        b_parts = [table[i * SIDE + j : i * SIDE + j + 1, half:] for i in range(SIDE)]
        row = jnp.concatenate(a_parts + b_parts, axis=1)
        size, at = row.shape[1], ORDER[j]
        total_ref[:, at * size : (at + 1) * size] = row
    log_ref[...] = table[0:1] * math.log(2.0)


def spread(own, came):
    groups, anchors = own.shape
    return pl.pallas_call(
        spread_kernel,
        out_shape=(
            jax.ShapeDtypeStruct((1, groups * anchors), F32),
            jax.ShapeDtypeStruct((1, anchors), F32),
        ),
        compiler_params=params(8),
        name="level_spread",
    )(own, *came)


def combine_kernel(total_ref, *refs):
    piece_refs, out_refs = refs[: 2 * SIDE], refs[2 * SIDE :]
    rows = piece_refs[0].shape[0] - LABEL
    half = rows // SIDE
    for h in range(2):
        total = total_ref[:, h * rows : (h + 1) * rows]
        joined = 0.0
        for ref in piece_refs[h * SIDE : (h + 1) * SIDE]:
            label = ref[rows:, :rows].astype(F32)
            level = label[0:1] + label[4:5] + label[8:9]
            factor = jnp.broadcast_to(jnp.exp2(level - total), (8, rows)).T[:, :1]
            joined = joined + ref[:rows, :].astype(F32) * factor
        for d in range(SIDE):
            out_ref = out_refs[h * SIDE + d]
            out_ref[...] = joined[d * half : (d + 1) * half].astype(out_ref.dtype)


def combine(total, pieces):
    rows, width = pieces[0].shape
    half = (rows - LABEL) // SIDE
    one = tuple(jax.ShapeDtypeStruct((half, width), F32 if d == 0 else BF) for d in range(SIDE))
    return pl.pallas_call(
        combine_kernel,
        out_shape=one + one,
        compiler_params=params(40),
        name="combine",
    )(total, *pieces)


def body(anchor_hidden, candidates, memory, anchor_ids, pos_ids, pos_count, snapshot):
    anchors, width = anchor_hidden.shape
    scale = 1.0 / math.sqrt(width)
    unit = scale * math.log2(math.e)
    half = anchors // 2
    steps = (1, 2, 3)

    along_y = [shift_y(candidates, d) for d in steps]

    ids = jnp.concatenate([anchor_ids[:, None], pos_ids], axis=1)
    requests, place = plan(ids.T, ids)
    asked = lax.all_to_all(requests, ("row", "col"), split_axis=0, concat_axis=0, tiled=True)
    asked, *along_y = lax.optimization_barrier((asked, *along_y))
    along_y = jnp.concatenate([candidates] + along_y, axis=0)
    near, far = along_y, swap_core(along_y)
    served = serve(asked, lax.dynamic_slice_in_dim(memory, snapshot[0], 2, 0))
    devices = asked.shape[0]
    served = served.reshape(devices, MAIN, served.shape[1])
    got = lax.all_to_all(served, ("row", "col"), split_axis=0, concat_axis=0, tiled=True)
    got = got.reshape(devices * MAIN, got.shape[2])
    query, positive, pos_logit = unpack(got, place, anchor_hidden, pos_count[:, None], scale)
    pos_logit = pos_logit.reshape(anchors)

    first, second = query[:half], query[half:]
    first = jnp.concatenate([first] + [shift_z(first, d) for d in steps], axis=0)
    second = jnp.concatenate([second] + [shift_x(second, d) for d in steps], axis=0)
    first, second = lax.optimization_barrier((first, second))
    came = {d: [shift_x(first, d), shift_z(second, d)] for d in (1, 3)}
    own = score(near, far, [first, second], unit)
    own_level, first, second, *came_13 = lax.optimization_barrier((own[1], first, second, *came[1], *came[3]))
    far_pieces = [shift_x(first, 2), shift_z(second, 2)]
    sides = score(near, far, came_13, unit)
    side_level, *far_pieces = lax.optimization_barrier((sides[1], *far_pieces))
    last = score(near, far, far_pieces, unit)
    sent = {1: list(sides[3:5]), 3: list(sides[5:7]), 2: list(last[3:5])}
    own_a, own_b = own[3:]
    logits, queries = (own[0], sides[0], last[0]), (own[2], sides[2], last[2])
    levels = (own_level, side_level, last[1])

    known = table(levels, pos_logit.reshape(1, anchors), anchors)
    known = merged(known, [shift_z(known, d) for d in steps], False)
    total, log_total = spread(known, [shift_x(known, d) for d in steps])
    log_total = log_total.reshape(anchors)

    total, *sides = lax.optimization_barrier((total, *sent[1], *sent[3]))
    sent[1], sent[3] = sides[:2], sides[2:]
    a_came = {d: shift_x(sent[d][0], -d) for d in (1, 3)}
    b_came = {d: shift_z(sent[d][1], -d) for d in (1, 3)}
    count = near.shape[0]
    away = cand_terms(logits, total, queries, count, count, BF, unit)
    total, away, *sent[2] = lax.optimization_barrier((total, away, *sent[2]))
    a_came[2], b_came[2] = shift_x(sent[2][0], -2), shift_z(sent[2][1], -2)
    came = swap_core(away)
    home = home_terms(logits, total, queries, came, unit)
    _, a_came[1], b_came[1], a_came[3], b_came[3] = lax.optimization_barrier(
        (home[0], a_came[1], b_came[1], a_came[3], b_came[3])
    )
    moved = [shift_y(home[d], -d) for d in steps]
    total, moved[0] = lax.optimization_barrier((total, moved[0]))
    cand_grad = home[0]
    for one in moved:
        cand_grad = cand_grad + one.astype(F32)

    summed = combine(total, [own_a] + [a_came[d] for d in steps] + [own_b] + [b_came[d] for d in steps])
    a_all, b_all = summed[0], summed[SIDE]
    for d in steps:
        a_all = a_all + shift_z(summed[d], -d).astype(F32)
        b_all = b_all + shift_x(summed[SIDE + d], -d).astype(F32)
    weighted = jnp.concatenate([a_all, b_all], axis=0)
    anchor_grad = weighted + (jnp.exp(pos_logit - log_total) - 1.0)[:, None] * positive.astype(F32)
    loss = log_total - pos_logit

    return (loss, anchor_grad, cand_grad)


def solution(mesh):
    in_specs = (
        P(("row", "col"), None),
        P(("col", "row"), None),
        P(None, ("row", "col"), None),
        P(("row", "col")),
        P(("row", "col"), None),
        P(("row", "col")),
        P(),
    )
    out_specs = (P(("row", "col")), P(("row", "col"), None), P(("col", "row"), None))
    return jax.shard_map(body, mesh=mesh, in_specs=in_specs, out_specs=out_specs, check_vma=False)
```

```python
import functools
import math

import jax
import jax.numpy as jnp
from jax import lax
from jax.experimental import pallas as pl
from jax.experimental.pallas import tpu as pltpu
from jax.sharding import PartitionSpec as P

BF = jnp.bfloat16
F32 = jnp.float32
I32 = jnp.int32
SIDE = 4
MIB = 1024 * 1024
MAIN = 8
SPARE = 4
TILE = 512
CHUNK = 256
LABEL = 16
ORDER = (0, 1, 3, 2)


def params(mib):
    return pltpu.CompilerParams(vmem_limit_bytes=mib * MIB)


def cost(flops, moved, exps=0):
    return pl.CostEstimate(flops=1, bytes_accessed=1, transcendentals=0)


def nn(a, b):
    return jnp.dot(a, b, preferred_element_type=F32)


def shift_x(value, by):
    pairs = [(x * SIDE + z, (x + by) % SIDE * SIDE + z) for x in range(SIDE) for z in range(SIDE)]
    return lax.ppermute(value, "row", pairs)


def shift_z(value, by):
    pairs = [(x * SIDE + z, x * SIDE + (z + by) % SIDE) for x in range(SIDE) for z in range(SIDE)]
    return lax.ppermute(value, "row", pairs)


def shift_y(value, by):
    pairs = [(y * 2 + k, (y + by) % SIDE * 2 + k) for y in range(SIDE) for k in range(2)]
    return lax.ppermute(value, "col", pairs)


def swap_core(value):
    return lax.ppermute(value, "col", [(i, i ^ 1) for i in range(2 * SIDE)])


def plan_kernel(rows_ref, cols_ref, request_ref, place_ref):
    rows, cols = rows_ref[...], cols_ref[...]
    kinds, anchors = rows.shape
    total = kinds * anchors
    across = jnp.concatenate([rows[k : k + 1, :] for k in range(kinds)], axis=1)
    down = jnp.concatenate([cols[:, k : k + 1] for k in range(kinds)], axis=0)
    owner_across = jnp.where(across >= 0, across >> 10, -1)
    owner_down = jnp.where(down >= 0, down >> 10, -2)
    first = lax.broadcasted_iota(I32, (total, total), 0)
    second = lax.broadcasted_iota(I32, (total, total), 1)
    same = (owner_down == owner_across) & (second < first)
    slot = jnp.sum(jnp.where(same, 1.0, 0.0), axis=1, keepdims=True).astype(I32)
    kind = jnp.where(lax.broadcasted_iota(I32, (total, 1), 0) < anchors, 0, 1024)
    code = (down & 1023) + kind + 1
    hit = (slot == lax.broadcasted_iota(I32, (total, 128), 1)) & (down >= 0)
    low = jnp.where(hit, code & 63, 0).astype(F32).astype(BF)
    high = jnp.where(hit, code >> 6, 0).astype(F32).astype(BF)
    devices = request_ref.shape[0]
    pick = jnp.where(owner_across == lax.broadcasted_iota(I32, (devices, total), 0), 1.0, 0.0).astype(BF)
    found = nn(pick, low) + 64.0 * nn(pick, high) - 1.0
    request_ref[...] = found[:, : request_ref.shape[1]].astype(I32)
    place = jnp.where(down >= 0, owner_down * 16 + slot, -1)
    for k in range(kinds):
        place_ref[:, k : k + 1] = place[k * anchors : (k + 1) * anchors]


def plan(rows, cols):
    return pl.pallas_call(
        plan_kernel,
        out_shape=(jax.ShapeDtypeStruct((128, 16), I32), jax.ShapeDtypeStruct(cols.shape, I32)),
        compiler_params=params(16),
        name="plan",
    )(rows, cols)


def serve_kernel(asked_ref, memory_ref, out_ref):
    asked = asked_ref[...]
    devices, lanes = asked.shape
    nodes, width = memory_ref.shape[1:]

    def rows_of(first, slots):
        count = devices * slots
        wide = jnp.broadcast_to(asked[:, None, :], (devices, slots, lanes)).reshape(count, lanes)
        lane = lax.broadcasted_iota(I32, (count, lanes), 1)
        spot = lax.broadcasted_iota(I32, (count, lanes), 0) & (slots - 1)
        code = jnp.sum(jnp.where(lane == first + spot, wide, 0), axis=1, keepdims=True)
        node = lax.broadcasted_iota(I32, (count, nodes), 1)
        now = jnp.where(node == code, 1.0, 0.0).astype(BF)
        later = jnp.where(node + nodes == code, 1.0, 0.0).astype(BF)
        return (nn(now, memory_ref[0]) + nn(later, memory_ref[1])).astype(BF)

    out_ref[:, :width] = rows_of(0, MAIN)
    extra = rows_of(MAIN, SPARE)
    half = width // 2
    row = lax.broadcasted_iota(I32, (devices * MAIN, devices * SPARE), 0)
    column = lax.broadcasted_iota(I32, (devices * MAIN, devices * SPARE), 1)
    spot = row & (MAIN - 1)
    match = (row >> 3) * SPARE + (spot & (SPARE - 1)) == column
    upper = jnp.where(match & (spot < SPARE), 1.0, 0.0).astype(BF)
    lower = jnp.where(match & (spot >= SPARE), 1.0, 0.0).astype(BF)
    out_ref[:, width:] = (nn(upper, extra[:, :half]) + nn(lower, extra[:, half:])).astype(BF)


def serve(asked, memory):
    devices, lanes = asked.shape
    _, nodes, width = memory.shape
    step = 64
    return pl.pallas_call(
        serve_kernel,
        grid=(devices // step,),
        in_specs=[
            pl.BlockSpec((step, lanes), lambda i: (i, 0)),
            pl.BlockSpec(memory.shape, lambda i: (0, 0, 0)),
        ],
        out_specs=pl.BlockSpec((step * MAIN, width + width // 2), lambda i: (i, 0)),
        out_shape=jax.ShapeDtypeStruct((devices * MAIN, width + width // 2), BF),
        compiler_params=params(36),
        name="serve",
    )(asked, memory)


def unpack_kernel(scale, got_ref, place_ref, hidden_ref, count_ref, query_ref, positive_ref, logit_ref):
    anchors, kinds = place_ref.shape
    total, wide = got_ref.shape
    width = hidden_ref.shape[1]
    spot = lax.broadcasted_iota(I32, (anchors, total), 1)

    def masks(k):
        place = place_ref[:, k : k + 1]
        base, slot = (place >> 4) * MAIN, place & 15
        live = place >= 0
        main = jnp.where(live & (slot < MAIN), base + slot, -1)
        upper = jnp.where(live & (slot >= MAIN), base + slot - MAIN, -1)
        lower = jnp.where(live & (slot >= MAIN), base + slot - MAIN + SPARE, -1)
        return [jnp.where(spot == at, 1.0, 0.0) for at in (main, upper, lower)]

    first = masks(0)
    others = masks(1)
    for k in range(2, kinds):
        others = [a + b for a, b in zip(others, masks(k))]
    picks = [jnp.concatenate([a, b], axis=0).astype(BF) for a, b in zip(first, others)]
    rows = nn(picks[0], got_ref[:, :width])
    tail = got_ref[:, width:]
    rows = rows + jnp.concatenate([nn(picks[1], tail), nn(picks[2], tail)], axis=1)
    query = (hidden_ref[...].astype(F32) + rows[:anchors]).astype(BF)
    positive = (rows[anchors:] / count_ref[...].astype(F32)).astype(BF)
    query_ref[...] = query
    positive_ref[...] = positive
    logit_ref[...] = jnp.sum(query.astype(F32) * positive.astype(F32), axis=1, keepdims=True) * scale


def unpack(got, place, hidden, count, scale):
    anchors, width = hidden.shape
    return pl.pallas_call(
        functools.partial(unpack_kernel, scale),
        out_shape=(
            jax.ShapeDtypeStruct((anchors, width), BF),
            jax.ShapeDtypeStruct((anchors, width), BF),
            jax.ShapeDtypeStruct((anchors, 1), F32),
        ),
        compiler_params=params(16),
        name="unpack",
    )(got, place, hidden, count)


def score_kernel(unit, near_ref, far_ref, *refs):
    pieces = (len(refs) - 4) // 2
    piece_refs, (logit_ref, level_ref, query_ref) = refs[:pieces], refs[pieces : pieces + 3]
    sent_refs, sems = refs[pieces + 3 : -1], refs[-1]
    step = pl.program_id(0)
    size = piece_refs[0].shape[0]
    copies = [
        pltpu.make_async_copy(ref, query_ref.at[pl.ds(k * size, size), :], sems.at[k])
        for k, ref in enumerate(piece_refs)
    ]

    @pl.when(step == 0)
    def _():
        for copy in copies:
            copy.start()

    for g in range(len(copies) // 2):

        @pl.when(step == g)
        def _():
            copies[2 * g].wait()
            copies[2 * g + 1].wait()

    queries = query_ref[pl.ds(pl.multiple_of(step * 2 * size, 2 * size), 2 * size), :]
    count = near_ref.shape[0]
    chunks = [(ref, row) for ref in (near_ref, far_ref) for row in range(0, count, CHUNK)]
    top = None
    for j, (ref, row) in enumerate(chunks):
        logits = lax.dot_general(
            ref[row : row + CHUNK, :], queries, (((1,), (1,)), ((), ())), preferred_element_type=F32
        )
        logit_ref[j * CHUNK : (j + 1) * CHUNK, :] = logits
        peak = jnp.max(logits, axis=0, keepdims=True)
        top = peak if top is None else jnp.maximum(top, peak)
    top = top * unit
    total, weights = 0.0, []
    for j in range(len(chunks)):
        one = jnp.exp2(logit_ref[j * CHUNK : (j + 1) * CHUNK, :] * unit - top)
        total = total + jnp.sum(one, axis=0, keepdims=True)
        weights.append(one.astype(BF))
    half = len(weights) // 2
    part = 0.0
    for ref, some in ((near_ref, weights[:half]), (far_ref, weights[half:])):
        turned = (((0,), (0,)), ((), ()))
        part = part + lax.dot_general(jnp.concatenate(some, axis=0), ref[...], turned, preferred_element_type=F32)
    level_ref[...] = top + jnp.log2(total)
    part, width = part.astype(BF), part.shape[1]
    blank = jnp.zeros((LABEL, width - size), F32)
    for g in range(pieces // 2):

        @pl.when(step == g)
        def _():
            for h in range(2):
                cut = slice(h * size, (h + 1) * size)
                label = split_rows(top[:, cut])
                sent_refs[2 * g + h][:size, :] = part[cut]
                sent_refs[2 * g + h][size:, :] = jnp.concatenate([label, blank], axis=1).astype(BF)


def split_rows(level):
    high = level.astype(BF).astype(F32)
    middle = (level - high).astype(BF).astype(F32)
    low = level - high - middle
    row = lax.broadcasted_iota(I32, (LABEL, level.shape[1]), 0)
    return jnp.where(row < 4, high, jnp.where(row < 8, middle, low))


def score(near, far, pieces, unit, mib):
    cand_count, width = 2 * near.shape[0], near.shape[1]
    groups, each = len(pieces) // 2, 2 * pieces[0].shape[0]
    anchors = groups * each
    pairs = cand_count * anchors
    return pl.pallas_call(
        functools.partial(score_kernel, unit),
        grid=(groups,),
        in_specs=[pl.BlockSpec(memory_space=pltpu.VMEM)] * 2
        + [pl.BlockSpec(memory_space=pltpu.HBM) for _ in pieces],
        out_specs=(
            pl.BlockSpec((cand_count, each), lambda i: (0, i)),
            pl.BlockSpec((1, each), lambda i: (0, i)),
            pl.BlockSpec((anchors, width), lambda i: (0, 0)),
        )
        + (pl.BlockSpec((each // 2 + LABEL, width), lambda i: (0, 0)),) * len(pieces),
        out_shape=(
            pltpu.HBM((cand_count, anchors), F32),
            jax.ShapeDtypeStruct((1, anchors), F32),
            jax.ShapeDtypeStruct((anchors, width), BF),
        )
        + (jax.ShapeDtypeStruct((each // 2 + LABEL, width), BF),) * len(pieces),
        scratch_shapes=[pltpu.SemaphoreType.DMA((len(pieces),))],
        compiler_params=params(mib),
        cost_estimate=cost(4 * pairs * width, 4 * pairs, pairs),
        name="score",
    )(near, far, *pieces)


def cand_kernel(unit, *refs):
    arrays = (len(refs) - 2) // 2
    logit_refs, total_ref, query_refs, part_ref = refs[:arrays], refs[arrays], refs[arrays + 1 : -1], refs[-1]
    part, start = 0.0, 0
    for logit_ref, query_ref in zip(logit_refs, query_refs):
        stop = start + logit_ref.shape[1]
        weights = jnp.exp2(logit_ref[...] * unit - total_ref[:, start:stop]).astype(BF)
        part = part + nn(weights, query_ref[...])
        start = stop
    part_ref[...] = part.astype(part_ref.dtype)


def cand_terms(logits, total, queries, first, count, kind, unit):
    width = queries[0].shape[1]
    anchors = total.shape[1]
    start = first // TILE
    pairs = count * anchors
    return pl.pallas_call(
        functools.partial(cand_kernel, unit),
        grid=(count // TILE,),
        in_specs=[pl.BlockSpec((TILE, part.shape[1]), lambda i: (i + start, 0)) for part in logits]
        + [pl.BlockSpec((1, anchors), lambda i: (0, 0))]
        + [pl.BlockSpec(part.shape, lambda i: (0, 0)) for part in queries],
        out_specs=pl.BlockSpec((TILE, width), lambda i: (i, 0)),
        out_shape=jax.ShapeDtypeStruct((count, width), kind),
        compiler_params=params(60),
        cost_estimate=cost(2 * pairs * width, 4 * pairs, pairs),
        name="cand_terms",
    )(*logits, total, *queries)


def home_kernel(unit, *refs):
    arrays = (len(refs) - 6) // 2
    logit_refs, total_ref, query_refs = refs[:arrays], refs[arrays], refs[arrays + 1 : -5]
    came_ref, out_refs = refs[-5], refs[-4:]
    part, start = came_ref[...].astype(F32), 0
    for logit_ref, query_ref in zip(logit_refs, query_refs):
        stop = start + logit_ref.shape[1]
        weights = jnp.exp2(logit_ref[...] * unit - total_ref[:, start:stop]).astype(BF)
        part = part + nn(weights, query_ref[...])
        start = stop
    shard = out_refs[0].shape[0]
    each = part.shape[0] // shard
    for d, out_ref in enumerate(out_refs):

        @pl.when(pl.program_id(0) == d // each)
        def _():
            row = d % each * shard
            out_ref[...] = part[row : row + shard].astype(out_ref.dtype)


def home_terms(logits, total, queries, came, unit):
    count, width = came.shape
    anchors = total.shape[1]
    return pl.pallas_call(
        functools.partial(home_kernel, unit),
        grid=(count // TILE,),
        in_specs=[pl.BlockSpec((TILE, part.shape[1]), lambda i: (i, 0)) for part in logits]
        + [pl.BlockSpec((1, anchors), lambda i: (0, 0))]
        + [pl.BlockSpec(part.shape, lambda i: (0, 0)) for part in queries]
        + [pl.BlockSpec((TILE, width), lambda i: (i, 0))],
        out_specs=(pl.BlockSpec((count // SIDE, width), lambda i: (0, 0)),) * SIDE,
        out_shape=tuple(jax.ShapeDtypeStruct((count // SIDE, width), F32 if d == 0 else BF) for d in range(SIDE)),
        compiler_params=params(60),
        cost_estimate=cost(1, 1),
        name="home_terms",
    )(*logits, total, *queries, came)


def merge(levels):
    top = functools.reduce(jnp.maximum, levels)
    return top + jnp.log2(sum(jnp.exp2(level - top) for level in levels))


def table_kernel(*refs):
    level_refs, (logit_ref, table_ref) = refs[:-2], refs[-2:]
    levels = jnp.concatenate([ref[...] for ref in level_refs], axis=1)
    half = table_ref.shape[1] // 2
    size = 2 * SIDE * half
    levels = jnp.concatenate([levels[:, j * size : (j + 1) * size] for j in ORDER], axis=1)
    rows = []
    for x in range(SIDE):
        for z in range(SIDE):
            a_part = levels[:, x * size + z * half : x * size + (z + 1) * half]
            b_part = levels[:, z * size + (SIDE + x) * half : z * size + (SIDE + x + 1) * half]
            rows.append(jnp.concatenate([a_part, b_part], axis=1))
    rows[0] = merge([rows[0], logit_ref[...] * math.log2(math.e)])
    table_ref[...] = jnp.concatenate(rows, axis=0)


def table(levels, pos_logit, anchors):
    return pl.pallas_call(
        table_kernel,
        out_shape=jax.ShapeDtypeStruct((SIDE * SIDE, anchors), F32),
        compiler_params=params(8),
        name="level_table",
    )(*levels, pos_logit)


def rolled(value, along_x, by):
    if along_x:
        cut = (SIDE - by) * SIDE
        return jnp.concatenate([value[cut:], value[:cut]], axis=0)
    rows = []
    for x in range(SIDE):
        cut = x * SIDE + SIDE - by
        rows += [value[cut : (x + 1) * SIDE], value[x * SIDE : cut]]
    return jnp.concatenate(rows, axis=0)


def merge_kernel(along_x, own_ref, *refs):
    came_refs, out_ref = refs[:-1], refs[-1]
    levels = [own_ref[...]]
    for by, ref in zip((1, 2, 3), came_refs):
        levels.append(rolled(ref[...], along_x, by))
    out_ref[...] = merge(levels)


def merged(own, came, along_x):
    return pl.pallas_call(
        functools.partial(merge_kernel, along_x),
        out_shape=jax.ShapeDtypeStruct(own.shape, F32),
        compiler_params=params(8),
        name="level_merge",
    )(own, *came)


def spread_kernel(own_ref, *refs):
    came_refs, (total_ref, log_ref) = refs[:3], refs[3:]
    levels = [own_ref[...]]
    for by, ref in zip((1, 2, 3), came_refs):
        levels.append(rolled(ref[...], True, by))
    table = merge(levels)
    half = table.shape[1] // 2
    for j in range(SIDE):
        a_parts = [table[j * SIDE + i : j * SIDE + i + 1, :half] for i in range(SIDE)]
        b_parts = [table[i * SIDE + j : i * SIDE + j + 1, half:] for i in range(SIDE)]
        row = jnp.concatenate(a_parts + b_parts, axis=1)
        size, at = row.shape[1], ORDER[j]
        total_ref[:, at * size : (at + 1) * size] = row
    log_ref[...] = table[0:1] * math.log(2.0)


def spread(own, came):
    groups, anchors = own.shape
    return pl.pallas_call(
        spread_kernel,
        out_shape=(
            jax.ShapeDtypeStruct((1, groups * anchors), F32),
            jax.ShapeDtypeStruct((1, anchors), F32),
        ),
        compiler_params=params(8),
        name="level_spread",
    )(own, *came)


def combine_kernel(total_ref, *refs):
    piece_refs, out_refs = refs[: 2 * SIDE], refs[2 * SIDE :]
    rows = piece_refs[0].shape[0] - LABEL
    half = rows // SIDE
    for h in range(2):
        total = total_ref[:, h * rows : (h + 1) * rows]
        joined = 0.0
        for ref in piece_refs[h * SIDE : (h + 1) * SIDE]:
            label = ref[rows:, :rows].astype(F32)
            level = label[0:1] + label[4:5] + label[8:9]
            factor = jnp.broadcast_to(jnp.exp2(level - total), (8, rows)).T[:, :1]
            joined = joined + ref[:rows, :].astype(F32) * factor
        for d in range(SIDE):
            out_ref = out_refs[h * SIDE + d]
            out_ref[...] = joined[d * half : (d + 1) * half].astype(out_ref.dtype)


def combine(total, pieces):
    rows, width = pieces[0].shape
    half = (rows - LABEL) // SIDE
    one = tuple(jax.ShapeDtypeStruct((half, width), F32 if d == 0 else BF) for d in range(SIDE))
    return pl.pallas_call(
        combine_kernel,
        out_shape=one + one,
        compiler_params=params(40),
        name="combine",
    )(total, *pieces)


def body(anchor_hidden, candidates, memory, anchor_ids, pos_ids, pos_count, snapshot):
    anchors, width = anchor_hidden.shape
    scale = 1.0 / math.sqrt(width)
    unit = scale * math.log2(math.e)
    half = anchors // 2
    steps = (1, 2, 3)

    along_y = [shift_y(candidates, d) for d in steps]

    ids = jnp.concatenate([anchor_ids[:, None], pos_ids], axis=1)
    requests, place = plan(ids.T, ids)
    asked = lax.all_to_all(requests, ("row", "col"), split_axis=0, concat_axis=0, tiled=True)
    asked, *along_y = lax.optimization_barrier((asked, *along_y))
    along_y = jnp.concatenate([candidates] + along_y, axis=0)
    near, far = along_y, swap_core(along_y)
    served = serve(asked, lax.dynamic_slice_in_dim(memory, snapshot[0], 2, 0))
    devices = asked.shape[0]
    served = served.reshape(devices, MAIN, served.shape[1])
    got = lax.all_to_all(served, ("row", "col"), split_axis=0, concat_axis=0, tiled=True)
    got = got.reshape(devices * MAIN, got.shape[2])
    query, positive, pos_logit = unpack(got, place, anchor_hidden, pos_count[:, None], scale)
    pos_logit = pos_logit.reshape(anchors)

    first, second = query[:half], query[half:]
    first = jnp.concatenate([first] + [shift_z(first, d) for d in steps], axis=0)
    second = jnp.concatenate([second] + [shift_x(second, d) for d in steps], axis=0)
    first, second = lax.optimization_barrier((first, second))
    came = {d: [shift_x(first, d), shift_z(second, d)] for d in (1, 3)}
    own = score(near, far, [first, second], unit, 56)
    own_level, first, second, *came_13 = lax.optimization_barrier((own[1], first, second, *came[1], *came[3]))
    far_pieces = [shift_x(first, 2), shift_z(second, 2)]
    sides = score(near, far, came_13, unit, 36)
    side_level, *far_pieces = lax.optimization_barrier((sides[1], *far_pieces))
    last = score(near, far, far_pieces, unit, 36)
    sent = {1: list(sides[3:5]), 3: list(sides[5:7]), 2: list(last[3:5])}
    own_a, own_b = own[3:]
    logits, queries = (own[0], sides[0], last[0]), (own[2], sides[2], last[2])
    levels = (own_level, side_level, last[1])

    known = table(levels, pos_logit.reshape(1, anchors), anchors)
    known = merged(known, [shift_z(known, d) for d in steps], False)
    total, log_total = spread(known, [shift_x(known, d) for d in steps])
    log_total = log_total.reshape(anchors)

    total, *sides = lax.optimization_barrier((total, *sent[1], *sent[3]))
    sent[1], sent[3] = sides[:2], sides[2:]
    a_came = {d: shift_x(sent[d][0], -d) for d in (1, 3)}
    b_came = {d: shift_z(sent[d][1], -d) for d in (1, 3)}
    count = near.shape[0]
    away = cand_terms(logits, total, queries, count, count, BF, unit)
    total, away = lax.optimization_barrier((total, away))
    came = swap_core(away)
    home = home_terms(logits, total, queries, came, unit)
    _, a_came[1], b_came[1], a_came[3], b_came[3], *sent[2] = lax.optimization_barrier(
        (home[0], a_came[1], b_came[1], a_came[3], b_came[3], *sent[2])
    )
    a_came[2], b_came[2] = shift_x(sent[2][0], -2), shift_z(sent[2][1], -2)
    moved = [shift_y(home[d], -d) for d in steps]
    total, moved[0] = lax.optimization_barrier((total, moved[0]))
    cand_grad = home[0]
    for one in moved:
        cand_grad = cand_grad + one.astype(F32)

    summed = combine(total, [own_a] + [a_came[d] for d in steps] + [own_b] + [b_came[d] for d in steps])
    a_all, b_all = summed[0], summed[SIDE]
    for d in steps:
        a_all = a_all + shift_z(summed[d], -d).astype(F32)
        b_all = b_all + shift_x(summed[SIDE + d], -d).astype(F32)
    weighted = jnp.concatenate([a_all, b_all], axis=0)
    anchor_grad = weighted + (jnp.exp(pos_logit - log_total) - 1.0)[:, None] * positive.astype(F32)
    loss = log_total - pos_logit

    return (loss, anchor_grad, cand_grad)


def solution(mesh):
    in_specs = (
        P(("row", "col"), None),
        P(("col", "row"), None),
        P(None, ("row", "col"), None),
        P(("row", "col")),
        P(("row", "col"), None),
        P(("row", "col")),
        P(),
    )
    out_specs = (P(("row", "col")), P(("row", "col"), None), P(("col", "row"), None))
    return jax.shard_map(body, mesh=mesh, in_specs=in_specs, out_specs=out_specs, check_vma=False)
```
